512 devices in a mesh: rep: 32 (over z, core), fsdp: 8 (over y, x_lo), tp: 2 (over x_hi).
Axes of the slice: x: 4 (x_hi: 2, x_lo: 2; x = x_hi * 2 + x_lo), y: 4, z: 16, core: 2. Of those that a mesh axis runs over, the one named last changes fastest.
Arguments:
- tokens: bfloat16 [32, 2, 5120, 512], P('rep', None, ('fsdp', 'tp')), may hold values from -6 to 6
- queries: bfloat16 [32, 2, 512, 4096], P('rep', None, 'fsdp', 'tp'), may hold values from -6 to 6
- cotangent: bfloat16 [32, 2, 512, 4096], P('rep', None, 'fsdp', 'tp'), may hold values from -6 to 6
- outer_weights: bfloat16 [32, 5120, 1024], P('rep', ('fsdp', 'tp')), may hold values from -4 to 4
- momentum: bfloat16 [32, 5120, 1024], P('rep', ('fsdp', 'tp')), may hold values from -3 to 3
- partner_mask: int32 [1], replicated, may hold values from 1 to 31
Outputs:
- new_weights: bfloat16 [32, 5120, 1024], P('rep', ('fsdp', 'tp'))
- new_momentum: bfloat16 [32, 5120, 1024], P('rep', ('fsdp', 'tp'))
The draws below stay inside these ranges and needn't reach their ends.
Inputs may be any that keep to these rules, and one draw needn't show every extreme that they name: `partner_mask`: replica r is paired with replica r XOR the mask.
All inputs are finite; a program needn't handle non-finite values.
Results may differ from the reference program's by a relative error of at most 0.03.
Values may be sent and summed in bfloat16 or wider, within the bound.
A program may use at most 64 MiB of HBM per device.

```python
import jax
import jax.numpy as jnp
from jax import lax

D = 5120
HD = 128
KVH = 4
GROUP = 8
STEPS = 2
TOK_DEV = 64
SEQ = 512
QH = 32
COLS = 1024
N_REP = 32
N_FSDP = 8
N_TP = 2


def block_levels(own_key, dims, pieces, smallest, top_value):
    level = 1.0
    for axis_at, shards_of in pieces:
        steps = jax.random.uniform(jax.random.fold_in(jax.random.fold_in(own_key, 6), axis_at), (shards_of,), jnp.float32, smallest / len(pieces), top_value / len(pieces))
        level = level * jnp.repeat(jnp.exp(steps), dims[axis_at] // shards_of).reshape((-1,) + (1,) * (len(dims) - 1 - axis_at))
    return level


def gaussian(key, extent, scale, most, cuts=(), kind=jnp.bfloat16):
    values = jax.random.normal(key, extent, jnp.float32) * scale
    if len(cuts) > 0:
        values = block_levels(key, extent, cuts, -0.22, 0.18) * values
    return jnp.clip(values, min=-most, max=most).astype(kind)


def setup_inputs(seed: int = 0) -> dict:
    splits = jax.random.split(jax.random.key(seed), 7)
    return {
        "tokens": gaussian(splits[0], (N_REP, STEPS, D, SEQ), 1.0, 6.0, ((0, 32), (2, 16))),
        "queries": gaussian(splits[1], (N_REP, STEPS, SEQ, QH * HD), 1.0, 6.0, ((0, 32), (2, 8), (3, 2))),
        "cotangent": gaussian(splits[2], (N_REP, STEPS, SEQ, QH * HD), 1.0, 6.0, ((0, 32), (2, 8), (3, 2))),
        "outer_weights": gaussian(splits[3], (N_REP, D, COLS), 1.0, 4.0, ((0, 32), (1, 16))),
        "momentum": gaussian(splits[4], (N_REP, D, COLS), 0.5, 3.0, ((0, 32), (1, 16))),
        "partner_mask": jax.random.randint(splits[5], (1,), 1, N_REP).astype(jnp.int32),
    }


EPSILON = 1e-06
INNER_RATE = 8.0
MOMENTUM_DECAY = 0.9
DELTA_WEIGHT = 0.35
PAIR_WEIGHT = 0.25

def rounded(value):
    return lax.optimization_barrier(value.astype(jnp.bfloat16)).astype(jnp.float32)

def column_scale(columns, model_width):
    half_cols = columns // 2
    return jnp.concatenate([jnp.ones((half_cols,), jnp.float32), jnp.full((half_cols,), model_width ** (-0.5), jnp.float32)])

def block_gradient(key_values, queries, cotangent, first_row):
    seq_len = key_values.shape[0]
    query_rows, groups, key_heads, head_size = queries.shape
    key_cols = key_heads * head_size
    key_full = key_values[:, :key_cols].astype(jnp.float32).reshape(seq_len, key_heads, head_size)
    value_full = key_values[:, key_cols:].astype(jnp.float32).reshape(seq_len, key_heads, head_size)
    key_norm = lax.rsqrt(lax.optimization_barrier(jnp.mean(key_full * key_full, axis=-1, keepdims=True)) + EPSILON)
    key_unit = key_full * key_norm
    key_low = rounded(key_unit)
    query_full = queries.astype(jnp.float32)
    query_low = rounded(query_full * lax.rsqrt(lax.optimization_barrier(jnp.mean(query_full * query_full, axis=-1, keepdims=True)) + EPSILON))
    cot_full = cotangent.astype(jnp.float32)
    scores = jnp.einsum('rgkd,skd->kgrs', query_low, key_low) * head_size ** (-0.5)
    position = first_row + jnp.arange(query_rows, dtype=jnp.int32)
    allowed = jnp.arange(seq_len, dtype=jnp.int32)[None, :] <= position[:, None]
    raised = jnp.where(allowed, jnp.exp(scores), 0.0)
    attention = raised / lax.optimization_barrier(jnp.sum(raised, axis=-1, keepdims=True))
    attention_low = rounded(attention)
    value_part = jnp.einsum('kgrs,rgkd->skd', attention_low, cot_full)
    prob_grad = jnp.einsum('rgkd,skd->kgrs', cot_full, value_full)
    score_grad = attention * (prob_grad - lax.optimization_barrier(jnp.sum(attention * prob_grad, axis=-1, keepdims=True)))
    score_low = rounded(score_grad * head_size ** (-0.5))
    unit_grad = jnp.einsum('kgrs,rgkd->skd', score_low, query_low)
    key_part = (unit_grad - key_unit * lax.optimization_barrier(jnp.mean(unit_grad * key_unit, axis=-1, keepdims=True))) * key_norm
    return jnp.concatenate([key_part.reshape(seq_len, key_cols), value_part.reshape(seq_len, key_cols)], axis=1)

def reference(tokens, queries, cotangent, outer_weights, momentum, partner_mask):
    blocks = N_FSDP * N_TP
    width = D // blocks
    columns = outer_weights.shape[2]
    scale = column_scale(columns, D)
    local_groups = GROUP // N_TP
    first_rows = jnp.arange(blocks, dtype=jnp.int32) // N_TP * TOK_DEV
    gradient_blocks = jax.vmap(block_gradient, in_axes=(None, 0, 0, 0))

    def to_blocks(array):
        shaped = array.reshape(N_FSDP, TOK_DEV, N_TP, local_groups, KVH, HD)
        return shaped.transpose(0, 2, 1, 3, 4, 5).reshape(blocks, TOK_DEV, local_groups, KVH, HD)

    def one_replica(inputs):
        features_all, query_all, cotangent_all, weights_low = inputs
        inner = weights_low.astype(jnp.float32)
        for inner_step in range(STEPS):
            features = features_all[inner_step]
            feature_blocks = features.astype(jnp.float32).reshape(blocks, width, SEQ)
            weight_blocks = rounded(inner).reshape(blocks, width, columns)
            block_terms = jnp.einsum('bds,bdc->bsc', feature_blocks, weight_blocks)
            key_values = (lax.optimization_barrier(jnp.sum(rounded(block_terms), axis=0)) * scale).astype(jnp.bfloat16)
            block_parts = gradient_blocks(key_values, to_blocks(query_all[inner_step]), to_blocks(cotangent_all[inner_step]), first_rows)
            kv_grad = lax.optimization_barrier(jnp.sum(rounded(block_parts), axis=0)).astype(jnp.bfloat16)
            update = jnp.dot(features, kv_grad, preferred_element_type=jnp.float32)
            inner = inner - INNER_RATE * (update * scale)
        return (weights_low.astype(jnp.float32) - inner).astype(jnp.bfloat16)
    weight_delta = lax.map(one_replica, (tokens, queries, cotangent, outer_weights))
    partner = jnp.bitwise_xor(jnp.arange(N_REP, dtype=jnp.int32), partner_mask[0])
    outer_full = outer_weights.astype(jnp.float32)
    delta_full = weight_delta.astype(jnp.float32)
    step_change = MOMENTUM_DECAY * momentum.astype(jnp.float32) - DELTA_WEIGHT * (delta_full + delta_full[partner]) - PAIR_WEIGHT * (outer_full - outer_full[partner])
    return ((outer_full + step_change).astype(jnp.bfloat16), step_change.astype(jnp.bfloat16))
```

```python
import functools

import jax
import jax.numpy as jnp
from jax import lax
from jax.experimental import pallas as pl
from jax.experimental.pallas import tpu as pltpu
from jax.sharding import PartitionSpec as P

D = 5120
HD = 128
KVH = 4
GROUP = 8
STEPS = 2

EPSILON = 1e-06
INNER_RATE = 8.0
MOMENTUM_DECAY = 0.9
DELTA_WEIGHT = 0.35
PAIR_WEIGHT = 0.25

MESH = pl.DeviceIdType.MESH
HOPS = 4
SKEW = 2
CHUNK = 128
VALUE_SCALE = D ** (-0.5)
HEAD_SCALE = HD ** (-0.5)


def neighbour_ids():
    rep, f, t = lax.axis_index("rep"), lax.axis_index("fsdp"), lax.axis_index("tp")
    x_lo, y = f % 2, f // 2
    y_lo, y_hi = y % 2, y // 2
    flip_x = f + 1 - 2 * x_lo
    flip_y_lo = f + 2 - 4 * y_lo
    ids = [
        (rep, flip_x, t),
        (rep, flip_x, 1 - t),
        (rep, flip_y_lo, t),
        (rep, 2 * (3 - y) + x_lo, t),
    ]
    bits = [(x_lo + t) % 2, t, (y_lo + y_hi) % 2, y_hi]
    return ids, bits


def front_kernel(
    tok_ref,
    query_ref,
    cot_in_ref,
    w_ref,
    payload_ref,
    delta_ref,
    theta,
    acc,
    gathered,
    landed,
    staged,
    query_low,
    cot,
    rs_send,
    rs_recv,
    ag_send,
    ag_recv,
):
    seq = tok_ref.shape[2]
    query_rows = query_ref.shape[1]
    groups = query_ref.shape[2] // (KVH * HD)
    lanes = groups * query_rows
    ids, bits = neighbour_ids()
    first_row = lax.axis_index("fsdp") * query_rows

    barrier = pltpu.get_barrier_semaphore()
    for other in ids:
        pl.semaphore_signal(barrier, inc=1, device_id=other, device_id_type=MESH)

    size = [seq >> (k + 1) for k in range(HOPS)]
    offset = [sum(size[:k]) for k in range(HOPS)]

    def dim(h, k):
        return (h + k) % HOPS

    base = []
    for h in range(KVH):
        starts = [jnp.int32(0)]
        for k in range(HOPS):
            starts.append(starts[-1] + bits[dim(h, k)] * size[k])
        base.append(starts)

    def rows(start, count):
        return pl.ds(pl.multiple_of(start, size[HOPS - 1]), count)

    def rs_copy(ar, h, k):
        part = (ar * KVH + h, pl.ds(offset[k], size[k]))
        return pltpu.make_async_remote_copy(
            src_ref=staged.at[part],
            dst_ref=landed.at[part],
            send_sem=rs_send.at[h, k],
            recv_sem=rs_recv.at[h, k],
            device_id=ids[dim(h, k)],
            device_id_type=MESH,
        )

    def ag_copy(ar, h, k):
        back = HOPS - 1 - k
        part = (ar * KVH + h, rows(base[h][back + 1], size[back]))
        return pltpu.make_async_remote_copy(
            src_ref=gathered.at[part],
            dst_ref=gathered.at[part],
            send_sem=ag_send.at[h, k],
            recv_sem=ag_recv.at[h, k],
            device_id=ids[dim(h, back)],
            device_id_type=MESH,
        )

    def begin_sum(ar, h):
        bit = bits[dim(h, 0)]
        n = size[0]
        staged[ar * KVH + h, pl.ds(offset[0], n)] = acc[h, rows((1 - bit) * n, n)].astype(jnp.bfloat16)
        rs_copy(ar, h, 0).start()

    def halve(ar, h, k):
        rs_copy(ar, h, k).wait()
        slot = ar * KVH + h
        start = base[h][k + 1]
        if k < HOPS - 1:
            n = size[k + 1]
            bit = bits[dim(h, k + 1)]
            gone, kept = (1 - bit) * n, bit * n
            total = acc[h, rows(start + gone, n)] + landed[slot, rows(offset[k] + gone, n)].astype(jnp.float32)
            staged[slot, pl.ds(offset[k + 1], n)] = total.astype(jnp.bfloat16)
            rs_copy(ar, h, k + 1).start()
            acc[h, rows(start + kept, n)] = acc[h, rows(start + kept, n)] + landed[
                slot, rows(offset[k] + kept, n)
            ].astype(jnp.float32)
        else:
            n = size[k]
            total = acc[h, rows(start, n)] + landed[slot, pl.ds(offset[k], n)].astype(jnp.float32)
            if ar % 2 == 0:
                total = jnp.concatenate([total[:, :HD], total[:, HD:] * VALUE_SCALE], axis=1)
            gathered[slot, rows(start, n)] = total.astype(jnp.bfloat16)
            ag_copy(ar, h, 0).start()

    def widen(ar, h, k):
        ag_copy(ar, h, k).wait()
        if k < HOPS - 1:
            ag_copy(ar, h, k + 1).start()

    def key_cols(h):
        return pl.ds(h * HD, HD)

    def value_cols(h):
        return pl.ds(KVH * HD + h * HD, HD)

    def project(s, h, low):
        acc[h] = lax.dot_general(
            tok_ref[s], low, (((0,), (0,)), ((), ())), preferred_element_type=jnp.float32
        )

    def prepare(s, h):
        for g in range(groups):
            cols = pl.ds((g * KVH + h) * HD, HD)
            q = query_ref[s, :, cols].astype(jnp.float32)
            norm = lax.rsqrt(jnp.mean(q * q, axis=-1, keepdims=True) + EPSILON)
            query_low[s, h, pl.ds(g * query_rows, query_rows)] = (q * norm).astype(jnp.bfloat16)
            cot[s, h, pl.ds(g * query_rows, query_rows)] = cot_in_ref[s, :, cols]

    def attend(s, h):
        slot = 2 * s * KVH + h
        q = query_low[s, h]
        c = cot[s, h]
        contract_last = (((1,), (1,)), ((), ()))
        position = first_row + lax.broadcasted_iota(jnp.int32, (CHUNK, lanes), 1) % query_rows
        row = lax.broadcasted_iota(jnp.int32, (CHUNK, lanes), 0)
        raised, prob_grad = [], []
        denom = jnp.zeros((1, lanes), jnp.float32)
        mixed = jnp.zeros((1, lanes), jnp.float32)
        units, norms = [], []
        for i in range(seq // CHUNK):
            part = pl.ds(i * CHUNK, CHUNK)
            keys = gathered[slot, part, :HD].astype(jnp.float32)
            norm = lax.rsqrt(jnp.mean(keys * keys, axis=-1, keepdims=True) + EPSILON)
            unit = keys * norm
            units.append(unit)
            norms.append(norm)
            scores = lax.dot_general(
                unit.astype(jnp.bfloat16), q, contract_last, preferred_element_type=jnp.float32
            )
            e = jnp.where(row + i * CHUNK <= position, jnp.exp(scores * HEAD_SCALE), 0.0)
            pg = lax.dot_general(
                gathered[slot, part, HD:], c, contract_last, preferred_element_type=jnp.float32
            )
            denom = denom + jnp.sum(e, axis=0, keepdims=True)
            mixed = mixed + jnp.sum(e * pg, axis=0, keepdims=True)
            raised.append(e)
            prob_grad.append(pg)
        inverse = 1.0 / denom
        mixed = mixed * inverse
        for i in range(seq // CHUNK):
            part = pl.ds(i * CHUNK, CHUNK)
            probs = raised[i] * inverse
            score_low = (probs * (prob_grad[i] - mixed) * HEAD_SCALE).astype(jnp.bfloat16)
            acc[h, part, HD:] = jnp.dot(probs.astype(jnp.bfloat16), c, preferred_element_type=jnp.float32)
            unit_grad = jnp.dot(score_low, q, preferred_element_type=jnp.float32)
            unit = units[i]
            acc[h, part, :HD] = (
                unit_grad - unit * jnp.mean(unit_grad * unit, axis=-1, keepdims=True)
            ) * norms[i]

    def descend(s, h):
        slot = (2 * s + 1) * KVH + h
        update = jnp.dot(tok_ref[s], gathered[slot], preferred_element_type=jnp.float32)
        scale = jnp.where(
            lax.broadcasted_iota(jnp.int32, (1, 2 * HD), 1) < HD, INNER_RATE, INNER_RATE * VALUE_SCALE
        )
        return theta[h] - update * scale

    def weights(h):
        return jnp.concatenate([w_ref[:, key_cols(h)], w_ref[:, value_cols(h)]], axis=1)

    def finish(h):
        low = weights(h).astype(jnp.float32)
        delta = (low - descend(STEPS - 1, h)).astype(jnp.bfloat16)
        payload = (PAIR_WEIGHT * low - DELTA_WEIGHT * delta.astype(jnp.float32)).astype(jnp.bfloat16)
        delta_ref[:, key_cols(h)] = delta[:, :HD]
        delta_ref[:, value_cols(h)] = delta[:, HD:]
        payload_ref[:, key_cols(h)] = payload[:, :HD]
        payload_ref[:, value_cols(h)] = payload[:, HD:]

    def task(h, index):
        ar, stage = index // (2 * HOPS), index % (2 * HOPS)
        if stage == 0:
            if ar > 0:
                widen(ar - 1, h, HOPS - 1)
            s = ar // 2
            if ar == 2 * STEPS:
                finish(h)
                return
            if ar % 2 == 1:
                attend(s, h)
            elif s == 0:
                low = weights(h)
                theta[h] = low.astype(jnp.float32)
                project(0, h, low)
            else:
                new = descend(s - 1, h)
                theta[h] = new
                project(s, h, new.astype(jnp.bfloat16))
            if ar == 0 and h == 0:
                pl.semaphore_wait(barrier, len(ids))
            begin_sum(ar, h)
            if ar % 2 == 0:
                prepare(s, h)
        elif stage <= HOPS:
            halve(ar, h, stage - 1)
        else:
            widen(ar, h, stage - HOPS - 1)

    last = 4 * HOPS * STEPS
    for tick in range(last + SKEW * (KVH - 1) + 1):
        for h in range(KVH):
            index = tick - SKEW * h
            if 0 <= index <= last:
                task(h, index)


def front(tokens, queries, cotangent, weights_low):
    steps, features, seq = tokens.shape
    columns = weights_low.shape[1]
    lanes = queries.shape[2] // (KVH * HD) * queries.shape[1]
    sums = 2 * steps * KVH
    vmem = pl.BlockSpec(memory_space=pltpu.VMEM)
    out = jax.ShapeDtypeStruct((features, columns), jnp.bfloat16)
    return pl.pallas_call(
        front_kernel,
        out_shape=(out, out),
        in_specs=[vmem] * 4,
        out_specs=(vmem, vmem),
        scratch_shapes=[
            pltpu.VMEM((KVH, features, 2 * HD), jnp.float32),
            pltpu.VMEM((KVH, seq, 2 * HD), jnp.float32),
            pltpu.VMEM((sums, seq, 2 * HD), jnp.bfloat16),
            pltpu.VMEM((sums, seq, 2 * HD), jnp.bfloat16),
            pltpu.VMEM((sums, seq, 2 * HD), jnp.bfloat16),
            pltpu.VMEM((steps, KVH, lanes, HD), jnp.bfloat16),
            pltpu.VMEM((steps, KVH, lanes, HD), jnp.bfloat16),
            pltpu.SemaphoreType.DMA((KVH, HOPS)),
            pltpu.SemaphoreType.DMA((KVH, HOPS)),
            pltpu.SemaphoreType.DMA((KVH, HOPS)),
            pltpu.SemaphoreType.DMA((KVH, HOPS)),
        ],
        compiler_params=pltpu.CompilerParams(
            collective_id=0, has_side_effects=True, vmem_limit_bytes=40 * 1024 * 1024
        ),
    )(tokens, queries, cotangent, weights_low)


def from_partner(value, mask_value):
    replicas = lax.axis_size("rep")

    def by(mask, value):
        return lax.ppermute(value, "rep", [(source, source ^ mask) for source in range(replicas)])

    return lax.switch(mask_value - 1, [functools.partial(by, mask) for mask in range(1, replicas)], value)


def on_device(tokens, queries, cotangent, outer_weights, momentum, partner_mask):
    weights_low = outer_weights[0]
    momentum_low = momentum[0]
    payload, weight_delta = front(tokens[0], queries[0], cotangent[0], weights_low)
    partner_payload = from_partner(payload, partner_mask[0])
    outer_full = weights_low.astype(jnp.float32)
    step_change = (
        MOMENTUM_DECAY * momentum_low.astype(jnp.float32)
        - DELTA_WEIGHT * weight_delta.astype(jnp.float32)
        - PAIR_WEIGHT * outer_full
        + partner_payload.astype(jnp.float32)
    )
    return (
        (outer_full + step_change).astype(jnp.bfloat16)[None],
        step_change.astype(jnp.bfloat16)[None],
    )


def solution(mesh):
    in_specs = (
        P("rep", None, ("fsdp", "tp"), None),
        P("rep", None, "fsdp", "tp"),
        P("rep", None, "fsdp", "tp"),
        P("rep", ("fsdp", "tp"), None),
        P("rep", ("fsdp", "tp"), None),
        P(),
    )
    out_specs = (P("rep", ("fsdp", "tp"), None), P("rep", ("fsdp", "tp"), None))
    return jax.shard_map(
        on_device, mesh=mesh, in_specs=in_specs, out_specs=out_specs, check_vma=False
    )
```

```python
import functools

import jax
import jax.numpy as jnp
from jax import lax
from jax.experimental import pallas as pl
from jax.experimental.pallas import tpu as pltpu
from jax.sharding import PartitionSpec as P

D = 5120
HD = 128
KVH = 4
GROUP = 8
STEPS = 2

EPSILON = 1e-06
INNER_RATE = 8.0
MOMENTUM_DECAY = 0.9
DELTA_WEIGHT = 0.35
PAIR_WEIGHT = 0.25

MESH = pl.DeviceIdType.MESH
RING = 4
SKEW = 0
VALUE_SCALE = D ** (-0.5)
HEAD_SCALE = HD ** (-0.5)


def ring_ids(axis):
    rep, f, t = lax.axis_index("rep"), lax.axis_index("fsdp"), lax.axis_index("tp")
    x, y = t * 2 + f % 2, f // 2
    if axis == 0:
        others = [(x + r) % RING for r in range(1, RING)]
        return x, [(rep, y * 2 + other % 2, other // 2) for other in others]
    others = [(y + r) % RING for r in range(1, RING)]
    return y, [(rep, other * 2 + f % 2, t) for other in others]


def front_kernel(
    tok_ref,
    query_ref,
    cot_in_ref,
    w_ref,
    payload_ref,
    delta_ref,
    theta,
    gathered,
    staged,
    landed,
    partial,
    crossed,
    query_low,
    cot,
    raised,
    prob_grad,
    units,
    norms,
    send_sem,
    recv_sem,
):
    seq = tok_ref.shape[2]
    query_rows = query_ref.shape[1]
    groups = query_ref.shape[2] // (KVH * HD)
    lanes = groups * query_rows
    block = seq // RING
    piece = block // RING
    rings = [ring_ids(0), ring_ids(1)]
    first_row = lax.axis_index("fsdp") * query_rows

    barrier = pltpu.get_barrier_semaphore()
    for _, ids in rings:
        for other in ids:
            pl.semaphore_signal(barrier, inc=1, device_id=other, device_id_type=MESH)

    def ring(h, phase):
        return rings[(h + phase) % 2]

    def rows(start, count):
        return pl.ds(pl.multiple_of(start, piece), count)

    def block_rows(h, r=0):
        return rows((ring(h, 0)[0] + r) % RING * block, block)

    def piece_rows(h, r=0):
        return rows((ring(h, 1)[0] + r) % RING * piece, piece)

    def own_piece(h):
        return rows(ring(h, 0)[0] * block + ring(h, 1)[0] * piece, piece)

    def copy(ar, h, stage, r):
        slot = ar * KVH + h
        if stage == 0:
            src, dst, phase = staged.at[slot, block_rows(h, r)], landed.at[slot, r - 1], 0
        elif stage == 1:
            src, dst, phase = partial.at[slot, piece_rows(h, r)], crossed.at[slot, r - 1], 1
        elif stage == 2:
            src = dst = gathered.at[slot, own_piece(h)]
            phase = 1
        else:
            src = dst = gathered.at[slot, block_rows(h)]
            phase = 0
        return pltpu.make_async_remote_copy(
            src_ref=src,
            dst_ref=dst,
            send_sem=send_sem.at[ar % 2, h, stage, r - 1],
            recv_sem=recv_sem.at[ar % 2, h, stage, r - 1],
            device_id=ring(h, phase)[1][r - 1],
            device_id_type=MESH,
        )

    def send(ar, h, stage):
        for r in range(1, RING):
            copy(ar, h, stage, r).start()

    def arrive(ar, h, stage):
        for r in range(1, RING):
            copy(ar, h, stage, r).wait()

    def first_sum(ar, h):
        arrive(ar, h, 0)
        slot = ar * KVH + h
        total = staged[slot, block_rows(h)].astype(jnp.float32)
        for r in range(1, RING):
            total = total + landed[slot, r - 1].astype(jnp.float32)
        partial[slot] = total.astype(jnp.bfloat16)
        send(ar, h, 1)

    def second_sum(ar, h):
        arrive(ar, h, 1)
        slot = ar * KVH + h
        total = partial[slot, piece_rows(h)].astype(jnp.float32)
        for r in range(1, RING):
            total = total + crossed[slot, r - 1].astype(jnp.float32)
        if ar % 2 == 0:
            total = jnp.concatenate([total[:, :HD], total[:, HD:] * VALUE_SCALE], axis=1)
        gathered[slot, own_piece(h)] = total.astype(jnp.bfloat16)
        send(ar, h, 2)

    def first_gather(ar, h):
        arrive(ar, h, 2)
        send(ar, h, 3)

    def key_cols(h):
        return pl.ds(h * HD, HD)

    def value_cols(h):
        return pl.ds(KVH * HD + h * HD, HD)

    def project(s, h, low):
        slot = 2 * s * KVH + h
        staged[slot] = lax.dot_general(
            tok_ref[s], low, (((0,), (0,)), ((), ())), preferred_element_type=jnp.float32
        ).astype(jnp.bfloat16)

    def prepare(s, h):
        for g in range(groups):
            cols = pl.ds((g * KVH + h) * HD, HD)
            q = query_ref[s, :, cols].astype(jnp.float32)
            norm = lax.rsqrt(jnp.mean(q * q, axis=-1, keepdims=True) + EPSILON)
            query_low[s, h, pl.ds(g * query_rows, query_rows)] = (q * norm).astype(jnp.bfloat16)
            cot[s, h, pl.ds(g * query_rows, query_rows)] = cot_in_ref[s, :, cols]

    def attend(s, h):
        slot = 2 * s * KVH + h
        q = query_low[s, h]
        c = cot[s, h]
        contract_last = (((1,), (1,)), ((), ()))
        position = first_row + lax.broadcasted_iota(jnp.int32, (block, lanes), 1) % query_rows
        row = lax.broadcasted_iota(jnp.int32, (block, lanes), 0)
        denom = jnp.zeros((1, lanes), jnp.float32)
        mixed = jnp.zeros((1, lanes), jnp.float32)
        for i in range(RING):
            part = pl.ds(i * block, block)
            keys = gathered[slot, part, :HD].astype(jnp.float32)
            norm = lax.rsqrt(jnp.mean(keys * keys, axis=-1, keepdims=True) + EPSILON)
            unit = keys * norm
            units[part] = unit
            norms[part] = jnp.broadcast_to(norm, unit.shape)
            scores = lax.dot_general(
                unit.astype(jnp.bfloat16), q, contract_last, preferred_element_type=jnp.float32
            )
            e = jnp.where(row + i * block <= position, jnp.exp(scores * HEAD_SCALE), 0.0)
            pg = lax.dot_general(
                gathered[slot, part, HD:], c, contract_last, preferred_element_type=jnp.float32
            )
            denom = denom + jnp.sum(e, axis=0, keepdims=True)
            mixed = mixed + jnp.sum(e * pg, axis=0, keepdims=True)
            raised[part] = e
            prob_grad[part] = pg
        inverse = 1.0 / denom
        mixed = mixed * inverse
        for r in (1, 2, 3, 0):
            part = block_rows(h, r)
            probs = raised[part] * inverse
            score_low = (probs * (prob_grad[part] - mixed) * HEAD_SCALE).astype(jnp.bfloat16)
            value_part = jnp.dot(probs.astype(jnp.bfloat16), c, preferred_element_type=jnp.float32)
            staged[slot + KVH, part, HD:] = value_part.astype(jnp.bfloat16)
            unit_grad = jnp.dot(score_low, q, preferred_element_type=jnp.float32)
            unit = units[part]
            key_part = (
                unit_grad - unit * jnp.mean(unit_grad * unit, axis=-1, keepdims=True)
            ) * norms[part]
            staged[slot + KVH, part, :HD] = key_part.astype(jnp.bfloat16)
            if r > 0:
                copy(2 * s + 1, h, 0, r).start()

    def descend(s, h):
        slot = (2 * s + 1) * KVH + h
        update = jnp.dot(tok_ref[s], gathered[slot], preferred_element_type=jnp.float32)
        scale = jnp.where(
            lax.broadcasted_iota(jnp.int32, (1, 2 * HD), 1) < HD, INNER_RATE, INNER_RATE * VALUE_SCALE
        )
        return theta[h] - update * scale

    def weights(h):
        return jnp.concatenate([w_ref[:, key_cols(h)], w_ref[:, value_cols(h)]], axis=1)

    def finish(h):
        low = weights(h).astype(jnp.float32)
        delta = (low - descend(STEPS - 1, h)).astype(jnp.bfloat16)
        payload = (PAIR_WEIGHT * low - DELTA_WEIGHT * delta.astype(jnp.float32)).astype(jnp.bfloat16)
        delta_ref[:, key_cols(h)] = delta[:, :HD]
        delta_ref[:, value_cols(h)] = delta[:, HD:]
        payload_ref[:, key_cols(h)] = payload[:, :HD]
        payload_ref[:, value_cols(h)] = payload[:, HD:]

    def task(h, index):
        ar, stage = index // 4, index % 4
        if stage == 0:
            if ar > 0:
                arrive(ar - 1, h, 3)
            s = ar // 2
            if ar == 2 * STEPS:
                finish(h)
                return
            if ar % 2 == 1:
                attend(s, h)
                return
            if s == 0:
                low = weights(h)
                theta[h] = low.astype(jnp.float32)
                project(0, h, low)
            else:
                new = descend(s - 1, h)
                theta[h] = new
                project(s, h, new.astype(jnp.bfloat16))
            if ar == 0 and h == 0:
                pl.semaphore_wait(barrier, 2 * (RING - 1))
            send(ar, h, 0)
            prepare(s, h)
        elif stage == 1:
            first_sum(ar, h)
        elif stage == 2:
            second_sum(ar, h)
        else:
            first_gather(ar, h)

    last = 8 * STEPS
    for tick in range(last + SKEW * (KVH - 1) + 1):
        for h in range(KVH):
            index = tick - SKEW * h
            if 0 <= index <= last:
                task(h, index)


def front(tokens, queries, cotangent, weights_low):
    steps, features, seq = tokens.shape
    columns = weights_low.shape[1]
    lanes = queries.shape[2] // (KVH * HD) * queries.shape[1]
    sums = 2 * steps * KVH
    vmem = pl.BlockSpec(memory_space=pltpu.VMEM)
    out = jax.ShapeDtypeStruct((features, columns), jnp.bfloat16)
    return pl.pallas_call(
        front_kernel,
        out_shape=(out, out),
        in_specs=[vmem] * 4,
        out_specs=(vmem, vmem),
        scratch_shapes=[
            pltpu.VMEM((KVH, features, 2 * HD), jnp.float32),
            pltpu.VMEM((sums, seq, 2 * HD), jnp.bfloat16),
            pltpu.VMEM((sums, seq, 2 * HD), jnp.bfloat16),
            pltpu.VMEM((sums, RING - 1, seq // RING, 2 * HD), jnp.bfloat16),
            pltpu.VMEM((sums, seq // RING, 2 * HD), jnp.bfloat16),
            pltpu.VMEM((sums, RING - 1, seq // RING // RING, 2 * HD), jnp.bfloat16),
            pltpu.VMEM((steps, KVH, lanes, HD), jnp.bfloat16),
            pltpu.VMEM((steps, KVH, lanes, HD), jnp.bfloat16),
            pltpu.VMEM((seq, lanes), jnp.float32),
            pltpu.VMEM((seq, lanes), jnp.float32),
            pltpu.VMEM((seq, HD), jnp.float32),
            pltpu.VMEM((seq, HD), jnp.float32),
            pltpu.SemaphoreType.DMA((2, KVH, 4, RING - 1)),
            pltpu.SemaphoreType.DMA((2, KVH, 4, RING - 1)),
        ],
        compiler_params=pltpu.CompilerParams(
            collective_id=0, has_side_effects=True, vmem_limit_bytes=40 * 1024 * 1024
        ),
    )(tokens, queries, cotangent, weights_low)


def from_partner(value, mask_value):
    replicas = lax.axis_size("rep")

    def by(mask, value):
        return lax.ppermute(value, "rep", [(source, source ^ mask) for source in range(replicas)])

    return lax.switch(mask_value - 1, [functools.partial(by, mask) for mask in range(1, replicas)], value)


def on_device(tokens, queries, cotangent, outer_weights, momentum, partner_mask):
    weights_low = outer_weights[0]
    momentum_low = momentum[0]
    payload, weight_delta = front(tokens[0], queries[0], cotangent[0], weights_low)
    partner_payload = from_partner(payload, partner_mask[0])
    outer_full = weights_low.astype(jnp.float32)
    step_change = (
        MOMENTUM_DECAY * momentum_low.astype(jnp.float32)
        - DELTA_WEIGHT * weight_delta.astype(jnp.float32)
        - PAIR_WEIGHT * outer_full
        + partner_payload.astype(jnp.float32)
    )
    return (
        (outer_full + step_change).astype(jnp.bfloat16)[None],
        step_change.astype(jnp.bfloat16)[None],
    )


def solution(mesh):
    in_specs = (
        P("rep", None, ("fsdp", "tp"), None),
        P("rep", None, "fsdp", "tp"),
        P("rep", None, "fsdp", "tp"),
        P("rep", ("fsdp", "tp"), None),
        P("rep", ("fsdp", "tp"), None),
        P(),
    )
    out_specs = (P("rep", ("fsdp", "tp"), None), P("rep", ("fsdp", "tp"), None))
    return jax.shard_map(
        on_device, mesh=mesh, in_specs=in_specs, out_specs=out_specs, check_vma=False
    )
```

```python
import functools

import jax
import jax.numpy as jnp
from jax import lax
from jax.experimental import pallas as pl
from jax.experimental.pallas import tpu as pltpu
from jax.sharding import PartitionSpec as P

D = 5120
HD = 128
KVH = 4
GROUP = 8
STEPS = 2

EPSILON = 1e-06
INNER_RATE = 8.0
MOMENTUM_DECAY = 0.9
DELTA_WEIGHT = 0.35
PAIR_WEIGHT = 0.25

MESH = pl.DeviceIdType.MESH
RING = 4
VALUE_SCALE = D ** (-0.5)
HEAD_SCALE = HD ** (-0.5)


class Plane:
    def __init__(self):
        self.rep, self.f, self.t = lax.axis_index("rep"), lax.axis_index("fsdp"), lax.axis_index("tp")
        self.x, self.y = self.t * 2 + self.f % 2, self.f // 2

    def place(self, ring):
        return self.x + (self.y - self.x) * ring

    def other(self, ring, r):
        x, y = (self.x + r) % RING, (self.y + r) % RING
        on_x, on_y = self.y * 2 + x % 2, y * 2 + self.f % 2
        return self.rep, on_x + (on_y - on_x) * ring, x // 2 + (self.t - x // 2) * ring

    def greet(self):
        barrier = pltpu.get_barrier_semaphore()
        for ring in range(2):
            for r in range(1, RING):
                pl.semaphore_signal(barrier, inc=1, device_id=self.other(ring, r), device_id_type=MESH)
        return barrier


def each(count, body):
    lax.fori_loop(0, count, lambda h, carry: (body(h), carry)[1], 0)


def key_cols(h):
    return pl.ds(pl.multiple_of(h * HD, HD), HD)


def value_cols(h):
    return pl.ds(pl.multiple_of(KVH * HD + h * HD, HD), HD)


def column_rate():
    column = lax.broadcasted_iota(jnp.int32, (1, 2 * HD), 1)
    return jnp.where(column < HD, INNER_RATE, INNER_RATE * VALUE_SCALE)


def inner_kernel(
    s,
    tok_hbm,
    query_hbm,
    cot_hbm,
    start_hbm,
    out_a,
    out_b,
    tok,
    query,
    cot_in,
    start,
    gathered,
    staged,
    landed,
    partial,
    crossed,
    query_low,
    cot,
    raised,
    prob_grad,
    units,
    norms,
    load_sem,
    send_sem,
    recv_sem,
):
    final = s == STEPS - 1
    seq = tok.shape[1]
    query_rows = query.shape[0]
    groups = query.shape[1] // (KVH * HD)
    lanes = groups * query_rows
    block = seq // RING
    piece = block // RING
    plane = Plane()
    first_row = plane.f * query_rows

    loads = [
        pltpu.make_async_copy(source, target, load_sem.at[i])
        for i, (source, target) in enumerate(
            [(start_hbm, start), (tok_hbm.at[s], tok), (query_hbm.at[s], query), (cot_hbm.at[s], cot_in)]
        )
    ]
    for load in loads:
        load.start()
    barrier = plane.greet()

    def rows(first, count):
        return pl.ds(pl.multiple_of(first, piece), count)

    def block_rows(h, r=0):
        return rows((plane.place(h % 2) + r) % RING * block, block)

    def piece_rows(h, r=0):
        return rows((plane.place(1 - h % 2) + r) % RING * piece, piece)

    def copy(ar, h, stage, r):
        slot = ar * KVH + h
        ring = h % 2
        if stage == 0:
            src, dst = staged.at[slot, block_rows(h, r)], landed.at[slot, r - 1]
        elif stage == 1 and final and ar == 1:
            src, dst = partial.at[slot, piece_rows(h, r)], crossed.at[slot, r - 1, pl.ds(0, piece)]
            ring = 1 - ring
        elif stage == 1:
            src, dst = partial.at[slot], crossed.at[slot, r - 1]
            ring = 1 - ring
        else:
            src = dst = gathered.at[slot, block_rows(h)]
        return pltpu.make_async_remote_copy(
            src_ref=src,
            dst_ref=dst,
            send_sem=send_sem.at[ar, h, stage, r - 1],
            recv_sem=recv_sem.at[ar, h, stage, r - 1],
            device_id=plane.other(ring, r),
            device_id_type=MESH,
        )

    def send(ar, h, stage):
        for r in range(1, RING):
            copy(ar, h, stage, r).start()

    def arrive(ar, h, stage):
        for r in range(1, RING):
            copy(ar, h, stage, r).wait()

    def project(h):
        if s == 0:
            low = jnp.concatenate([start[:, key_cols(h)], start[:, value_cols(h)]], axis=1)
        else:
            low = start[h].astype(jnp.bfloat16)
        staged[h] = lax.dot_general(
            tok[...], low, (((0,), (0,)), ((), ())), preferred_element_type=jnp.float32
        ).astype(jnp.bfloat16)
        send(0, h, 0)

    def prepare(h):
        for g in range(groups):
            cols = pl.ds(pl.multiple_of((g * KVH + h) * HD, HD), HD)
            q = query[:, cols].astype(jnp.float32)
            norm = lax.rsqrt(jnp.mean(q * q, axis=-1, keepdims=True) + EPSILON)
            query_low[h, pl.ds(g * query_rows, query_rows)] = (q * norm).astype(jnp.bfloat16)
            cot[h, pl.ds(g * query_rows, query_rows)] = cot_in[:, cols]

    def first_sum(ar, h):
        arrive(ar, h, 0)
        slot = ar * KVH + h
        total = staged[slot, block_rows(h)].astype(jnp.float32)
        for r in range(1, RING):
            total = total + landed[slot, r - 1].astype(jnp.float32)
        partial[slot] = total.astype(jnp.bfloat16)
        send(ar, h, 1)

    def second_sum(ar, h):
        arrive(ar, h, 1)
        slot = ar * KVH + h
        if final and ar == 1:
            total = partial[slot, piece_rows(h)].astype(jnp.float32)
            for r in range(1, RING):
                total = total + crossed[slot, r - 1, pl.ds(0, piece)].astype(jnp.float32)
            out_a[h] = total.astype(jnp.bfloat16)
            return
        total = partial[slot].astype(jnp.float32)
        for r in range(1, RING):
            total = total + crossed[slot, r - 1].astype(jnp.float32)
        if ar == 0:
            total = jnp.concatenate([total[:, :HD], total[:, HD:] * VALUE_SCALE], axis=1)
        gathered[slot, block_rows(h)] = total.astype(jnp.bfloat16)
        send(ar, h, 2)

    def attend(h):
        arrive(0, h, 2)
        q = query_low[h]
        c = cot[h]
        contract_last = (((1,), (1,)), ((), ()))
        position = first_row + lax.broadcasted_iota(jnp.int32, (block, lanes), 1) % query_rows
        row = lax.broadcasted_iota(jnp.int32, (block, lanes), 0)
        denom = jnp.zeros((1, lanes), jnp.float32)
        mixed = jnp.zeros((1, lanes), jnp.float32)
        for i in range(RING):
            part = pl.ds(i * block, block)
            keys = gathered[h, part, :HD].astype(jnp.float32)
            norm = lax.rsqrt(jnp.mean(keys * keys, axis=-1, keepdims=True) + EPSILON)
            unit = keys * norm
            units[part] = unit
            norms[part] = jnp.broadcast_to(norm, unit.shape)
            scores = lax.dot_general(
                unit.astype(jnp.bfloat16), q, contract_last, preferred_element_type=jnp.float32
            )
            e = jnp.where(row + i * block <= position, jnp.exp(scores * HEAD_SCALE), 0.0)
            pg = lax.dot_general(
                gathered[h, part, HD:], c, contract_last, preferred_element_type=jnp.float32
            )
            denom = denom + jnp.sum(e, axis=0, keepdims=True)
            mixed = mixed + jnp.sum(e * pg, axis=0, keepdims=True)
            raised[part] = e
            prob_grad[part] = pg
        inverse = 1.0 / denom
        mixed = mixed * inverse
        for r in (1, 2, 3, 0):
            part = block_rows(h, r)
            probs = raised[part] * inverse
            score_low = (probs * (prob_grad[part] - mixed) * HEAD_SCALE).astype(jnp.bfloat16)
            value_part = jnp.dot(probs.astype(jnp.bfloat16), c, preferred_element_type=jnp.float32)
            staged[KVH + h, part, HD:] = value_part.astype(jnp.bfloat16)
            unit_grad = jnp.dot(score_low, q, preferred_element_type=jnp.float32)
            unit = units[part]
            key_part = (
                unit_grad - unit * jnp.mean(unit_grad * unit, axis=-1, keepdims=True)
            ) * norms[part]
            staged[KVH + h, part, :HD] = key_part.astype(jnp.bfloat16)
            if r > 0:
                copy(1, h, 0, r).start()

    def descend(h):
        arrive(1, h, 2)
        change = jnp.dot(tok[...], gathered[KVH + h], preferred_element_type=jnp.float32) * column_rate()
        low = jnp.concatenate([start[:, key_cols(h)], start[:, value_cols(h)]], axis=1).astype(jnp.float32)
        out_a[h] = low - change
        payload = (PAIR_WEIGHT * low - DELTA_WEIGHT * change).astype(jnp.bfloat16)
        out_b[:, key_cols(h)] = payload[:, :HD]
        out_b[:, value_cols(h)] = payload[:, HD:]

    loads[0].wait()
    loads[1].wait()
    pl.semaphore_wait(barrier, 2 * (RING - 1))
    each(KVH, project)
    loads[2].wait()
    loads[3].wait()
    each(KVH, prepare)
    each(KVH, functools.partial(first_sum, 0))
    each(KVH, functools.partial(second_sum, 0))
    each(KVH, attend)
    each(KVH, functools.partial(first_sum, 1))
    each(KVH, functools.partial(second_sum, 1))
    if not final:
        each(KVH, descend)


def inner_step(s, tokens, queries, cotangent, start):
    steps, features, seq = tokens.shape
    rows, query_cols = queries.shape[1:]
    lanes = query_cols // (KVH * HD) * rows
    block = seq // RING
    any_space, vmem = pl.BlockSpec(memory_space=pl.ANY), pl.BlockSpec(memory_space=pltpu.VMEM)
    if s == 0:
        out_shape = (
            jax.ShapeDtypeStruct((KVH, features, 2 * HD), jnp.float32),
            jax.ShapeDtypeStruct((features, 2 * KVH * HD), jnp.bfloat16),
        )
        kernel = functools.partial(inner_kernel, s)
    else:
        out_shape = jax.ShapeDtypeStruct((KVH, block // RING, 2 * HD), jnp.bfloat16)

        def kernel(tok_hbm, query_hbm, cot_hbm, start_hbm, out, *scratch):
            inner_kernel(s, tok_hbm, query_hbm, cot_hbm, start_hbm, out, None, *scratch)

    return pl.pallas_call(
        kernel,
        out_shape=out_shape,
        in_specs=[any_space] * 4,
        out_specs=(vmem, vmem) if s == 0 else vmem,
        scratch_shapes=[
            pltpu.VMEM((features, seq), tokens.dtype),
            pltpu.VMEM((rows, query_cols), queries.dtype),
            pltpu.VMEM((rows, query_cols), cotangent.dtype),
            pltpu.VMEM(start.shape, start.dtype),
            pltpu.VMEM((2 * KVH, seq, 2 * HD), jnp.bfloat16),
            pltpu.VMEM((2 * KVH, seq, 2 * HD), jnp.bfloat16),
            pltpu.VMEM((2 * KVH, RING - 1, block, 2 * HD), jnp.bfloat16),
            pltpu.VMEM((2 * KVH, block, 2 * HD), jnp.bfloat16),
            pltpu.VMEM((2 * KVH, RING - 1, block, 2 * HD), jnp.bfloat16),
            pltpu.VMEM((KVH, lanes, HD), jnp.bfloat16),
            pltpu.VMEM((KVH, lanes, HD), jnp.bfloat16),
            pltpu.VMEM((seq, lanes), jnp.float32),
            pltpu.VMEM((seq, lanes), jnp.float32),
            pltpu.VMEM((seq, HD), jnp.float32),
            pltpu.VMEM((seq, HD), jnp.float32),
            pltpu.SemaphoreType.DMA((4,)),
            pltpu.SemaphoreType.DMA((2, KVH, 3, RING - 1)),
            pltpu.SemaphoreType.DMA((2, KVH, 3, RING - 1)),
        ],
        compiler_params=pltpu.CompilerParams(
            collective_id=s, has_side_effects=True, vmem_limit_bytes=32 * 1024 * 1024
        ),
    )(tokens, queries, cotangent, start)


def last_kernel(
    tok_hbm, partner_tok_hbm, theta_hbm, w_hbm, pieces_ref, partner_ref, out_ref,
    tok, partner_tok, theta, w, gathered, load_sem, send_sem, recv_sem,
):
    seq = tok.shape[1]
    block = seq // RING
    piece = block // RING
    plane = Plane()
    loads = [
        pltpu.make_async_copy(source, target, load_sem.at[i])
        for i, (source, target) in enumerate(
            [(tok_hbm.at[STEPS - 1], tok), (partner_tok_hbm, partner_tok), (theta_hbm, theta), (w_hbm, w)]
        )
    ]
    for load in loads:
        load.start()
    barrier = plane.greet()

    def rows(first, count):
        return pl.ds(pl.multiple_of(first, piece), count)

    def block_rows(h):
        return rows(plane.place(h % 2) * block, block)

    def own_piece(h):
        return rows(plane.place(h % 2) * block + plane.place(1 - h % 2) * piece, piece)

    def copy(h, stage, r):
        ring = 1 - h % 2 if stage == 0 else h % 2
        part = gathered.at[h, own_piece(h) if stage == 0 else block_rows(h)]
        return pltpu.make_async_remote_copy(
            src_ref=part,
            dst_ref=part,
            send_sem=send_sem.at[h, stage, r - 1],
            recv_sem=recv_sem.at[h, stage, r - 1],
            device_id=plane.other(ring, r),
            device_id_type=MESH,
        )

    def send(h, stage):
        for r in range(1, RING):
            copy(h, stage, r).start()

    def arrive(h, stage):
        for r in range(1, RING):
            copy(h, stage, r).wait()

    def begin(h):
        gathered[h, own_piece(h)] = pieces_ref[h]
        gathered[KVH + h, own_piece(h)] = partner_ref[h]
        send(h, 0)
        send(KVH + h, 0)

    def widen(h):
        arrive(h, 0)
        send(h, 1)

    def finish(h):
        arrive(h, 1)
        arrive(KVH + h, 1)
        change = jnp.dot(tok[...], gathered[h], preferred_element_type=jnp.float32) * column_rate()
        low = jnp.concatenate([w[:, key_cols(h)], w[:, value_cols(h)]], axis=1).astype(jnp.float32)
        delta = (low - (theta[h] - change)).astype(jnp.bfloat16).astype(jnp.float32)
        partner_change = (
            jnp.dot(partner_tok[...], gathered[KVH + h], preferred_element_type=jnp.float32) * column_rate()
        )
        total = delta + partner_change
        out_ref[:, key_cols(h)] = total[:, :HD]
        out_ref[:, value_cols(h)] = total[:, HD:]

    pl.semaphore_wait(barrier, 2 * (RING - 1))
    each(KVH, begin)
    each(2 * KVH, widen)
    for load in loads:
        load.wait()
    each(KVH, finish)


def last_step(tokens, partner_tokens, theta, weights_low, pieces, partner_pieces):
    steps, features, seq = tokens.shape
    any_space, vmem = pl.BlockSpec(memory_space=pl.ANY), pl.BlockSpec(memory_space=pltpu.VMEM)
    return pl.pallas_call(
        last_kernel,
        out_shape=jax.ShapeDtypeStruct(weights_low.shape, jnp.float32),
        in_specs=[any_space] * 4 + [vmem] * 2,
        out_specs=vmem,
        scratch_shapes=[
            pltpu.VMEM((features, seq), tokens.dtype),
            pltpu.VMEM((features, seq), tokens.dtype),
            pltpu.VMEM(theta.shape, theta.dtype),
            pltpu.VMEM(weights_low.shape, weights_low.dtype),
            pltpu.VMEM((2 * KVH, seq, 2 * HD), jnp.bfloat16),
            pltpu.SemaphoreType.DMA((4,)),
            pltpu.SemaphoreType.DMA((2 * KVH, 2, RING - 1)),
            pltpu.SemaphoreType.DMA((2 * KVH, 2, RING - 1)),
        ],
        compiler_params=pltpu.CompilerParams(
            collective_id=STEPS, has_side_effects=True, vmem_limit_bytes=32 * 1024 * 1024
        ),
    )(tokens, partner_tokens, theta, weights_low, pieces, partner_pieces)


def outer_step(exchange, tokens, queries, cotangent, weights_low, momentum_low):
    partner_tokens = exchange(tokens[STEPS - 1])
    theta, payload = inner_step(0, tokens, queries, cotangent, weights_low)
    partner_payload = exchange(payload)
    pieces = inner_step(1, tokens, queries, cotangent, theta)
    partner_pieces = exchange(pieces)
    moved = last_step(tokens, partner_tokens, theta, weights_low, pieces, partner_pieces)
    outer_full = weights_low.astype(jnp.float32)
    step_change = (
        MOMENTUM_DECAY * momentum_low.astype(jnp.float32)
        - DELTA_WEIGHT * moved
        - PAIR_WEIGHT * outer_full
        + partner_payload.astype(jnp.float32)
    )
    return (
        (outer_full + step_change).astype(jnp.bfloat16)[None],
        step_change.astype(jnp.bfloat16)[None],
    )


def on_device(tokens, queries, cotangent, outer_weights, momentum, partner_mask):
    replicas = lax.axis_size("rep")

    def by(mask, *arrays):
        pairs = [(source, source ^ mask) for source in range(replicas)]
        return outer_step(lambda value: lax.ppermute(value, "rep", pairs), *arrays)

    return lax.switch(
        partner_mask[0] - 1,
        [functools.partial(by, mask) for mask in range(1, replicas)],
        tokens[0],
        queries[0],
        cotangent[0],
        outer_weights[0],
        momentum[0],
    )


def solution(mesh):
    in_specs = (
        P("rep", None, ("fsdp", "tp"), None),
        P("rep", None, "fsdp", "tp"),
        P("rep", None, "fsdp", "tp"),
        P("rep", ("fsdp", "tp"), None),
        P("rep", ("fsdp", "tp"), None),
        P(),
    )
    out_specs = (P("rep", ("fsdp", "tp"), None), P("rep", ("fsdp", "tp"), None))
    return jax.shard_map(
        on_device, mesh=mesh, in_specs=in_specs, out_specs=out_specs, check_vma=False
    )
```

```python
import functools

import jax
import jax.numpy as jnp
from jax import lax
from jax.experimental import pallas as pl
from jax.experimental.pallas import tpu as pltpu
from jax.sharding import PartitionSpec as P

D = 5120
HD = 128
KVH = 4
GROUP = 8
STEPS = 2

EPSILON = 1e-06
INNER_RATE = 8.0
MOMENTUM_DECAY = 0.9
DELTA_WEIGHT = 0.35
PAIR_WEIGHT = 0.25

MESH = pl.DeviceIdType.MESH
RING = 4
SKEW = 0
FAR_FIRST = (2, 1, 3)
VALUE_SCALE = D ** (-0.5)
HEAD_SCALE = HD ** (-0.5)


def ring_ids(axis):
    rep, f, t = lax.axis_index("rep"), lax.axis_index("fsdp"), lax.axis_index("tp")
    x, y = t * 2 + f % 2, f // 2
    if axis == 0:
        others = [(x + r) % RING for r in range(1, RING)]
        return x, [(rep, y * 2 + other % 2, other // 2) for other in others]
    others = [(y + r) % RING for r in range(1, RING)]
    return y, [(rep, other * 2 + f % 2, t) for other in others]


def front_kernel(
    tok_hbm,
    query_hbm,
    cot_hbm,
    w_hbm,
    payload_ref,
    delta_ref,
    tok_ref,
    query_ref,
    cot_in_ref,
    w_ref,
    theta,
    gathered,
    staged,
    landed,
    partial,
    crossed,
    query_low,
    cot,
    raised,
    prob_grad,
    units,
    norms,
    load_sem,
    send_sem,
    recv_sem,
):
    seq = tok_ref.shape[2]
    query_rows = query_ref.shape[1]
    groups = query_ref.shape[2] // (KVH * HD)
    lanes = groups * query_rows
    block = seq // RING
    rings = [ring_ids(0), ring_ids(1)]
    first_row = lax.axis_index("fsdp") * query_rows

    pairs = [(w_hbm, w_ref)]
    for s in range(STEPS):
        pairs += [(a.at[s], b.at[s]) for a, b in ((tok_hbm, tok_ref), (query_hbm, query_ref), (cot_hbm, cot_in_ref))]
    loads = [pltpu.make_async_copy(a, b, load_sem.at[i]) for i, (a, b) in enumerate(pairs)]
    for load in loads:
        load.start()

    barrier = pltpu.get_barrier_semaphore()
    for _, ids in rings:
        for other in ids:
            pl.semaphore_signal(barrier, inc=1, device_id=other, device_id_type=MESH)

    def ring(h, phase):
        return rings[(h + phase) % 2]

    def block_rows(h, r=0):
        return pl.ds(pl.multiple_of((ring(h, 0)[0] + r) % RING * block, block), block)

    def copy(ar, h, stage, r):
        slot = ar * KVH + h
        if stage == 0:
            src, dst, phase = staged.at[slot, block_rows(h, r)], landed.at[slot, r - 1], 0
        elif stage == 1:
            src, dst, phase = partial.at[slot], crossed.at[slot, r - 1], 1
        else:
            src = dst = gathered.at[slot, block_rows(h)]
            phase = 0
        return pltpu.make_async_remote_copy(
            src_ref=src,
            dst_ref=dst,
            send_sem=send_sem.at[ar % 2, h, stage, r - 1],
            recv_sem=recv_sem.at[ar % 2, h, stage, r - 1],
            device_id=ring(h, phase)[1][r - 1],
            device_id_type=MESH,
        )

    def send(ar, h, stage):
        for r in FAR_FIRST:
            copy(ar, h, stage, r).start()

    def arrive(ar, h, stage):
        for r in range(1, RING):
            copy(ar, h, stage, r).wait()

    def first_sum(ar, h):
        arrive(ar, h, 0)
        slot = ar * KVH + h
        total = staged[slot, block_rows(h)].astype(jnp.float32)
        for r in range(1, RING):
            total = total + landed[slot, r - 1].astype(jnp.float32)
        partial[slot] = total.astype(jnp.bfloat16)
        send(ar, h, 1)

    def second_sum(ar, h):
        arrive(ar, h, 1)
        slot = ar * KVH + h
        total = partial[slot].astype(jnp.float32)
        for r in range(1, RING):
            total = total + crossed[slot, r - 1].astype(jnp.float32)
        if ar % 2 == 0:
            total = jnp.concatenate([total[:, :HD], total[:, HD:] * VALUE_SCALE], axis=1)
        gathered[slot, block_rows(h)] = total.astype(jnp.bfloat16)
        send(ar, h, 2)

    def key_cols(h):
        return pl.ds(h * HD, HD)

    def value_cols(h):
        return pl.ds(KVH * HD + h * HD, HD)

    def project(s, h, low):
        slot = 2 * s * KVH + h
        staged[slot] = lax.dot_general(
            tok_ref[s], low, (((0,), (0,)), ((), ())), preferred_element_type=jnp.float32
        ).astype(jnp.bfloat16)

    def prepare(s, h):
        for g in range(groups):
            cols = pl.ds((g * KVH + h) * HD, HD)
            q = query_ref[s, :, cols].astype(jnp.float32)
            norm = lax.rsqrt(jnp.mean(q * q, axis=-1, keepdims=True) + EPSILON)
            query_low[s, h, pl.ds(g * query_rows, query_rows)] = (q * norm).astype(jnp.bfloat16)
            cot[s, h, pl.ds(g * query_rows, query_rows)] = cot_in_ref[s, :, cols]

    def attend(s, h):
        slot = 2 * s * KVH + h
        q = query_low[s, h]
        c = cot[s, h]
        contract_last = (((1,), (1,)), ((), ()))
        position = first_row + lax.broadcasted_iota(jnp.int32, (block, lanes), 1) % query_rows
        row = lax.broadcasted_iota(jnp.int32, (block, lanes), 0)
        denom = jnp.zeros((1, lanes), jnp.float32)
        mixed = jnp.zeros((1, lanes), jnp.float32)
        for i in range(RING):
            part = pl.ds(i * block, block)
            keys = gathered[slot, part, :HD].astype(jnp.float32)
            norm = lax.rsqrt(jnp.mean(keys * keys, axis=-1, keepdims=True) + EPSILON)
            unit = keys * norm
            units[part] = unit
            norms[part] = jnp.broadcast_to(norm, unit.shape)
            scores = lax.dot_general(
                unit.astype(jnp.bfloat16), q, contract_last, preferred_element_type=jnp.float32
            )
            e = jnp.where(row + i * block <= position, jnp.exp(scores * HEAD_SCALE), 0.0)
            pg = lax.dot_general(
                gathered[slot, part, HD:], c, contract_last, preferred_element_type=jnp.float32
            )
            denom = denom + jnp.sum(e, axis=0, keepdims=True)
            mixed = mixed + jnp.sum(e * pg, axis=0, keepdims=True)
            raised[part] = e
            prob_grad[part] = pg
        inverse = 1.0 / denom
        mixed = mixed * inverse
        for r in FAR_FIRST + (0,):
            part = block_rows(h, r)
            probs = raised[part] * inverse
            score_low = (probs * (prob_grad[part] - mixed) * HEAD_SCALE).astype(jnp.bfloat16)
            value_part = jnp.dot(probs.astype(jnp.bfloat16), c, preferred_element_type=jnp.float32)
            staged[slot + KVH, part, HD:] = value_part.astype(jnp.bfloat16)
            unit_grad = jnp.dot(score_low, q, preferred_element_type=jnp.float32)
            unit = units[part]
            key_part = (
                unit_grad - unit * jnp.mean(unit_grad * unit, axis=-1, keepdims=True)
            ) * norms[part]
            staged[slot + KVH, part, :HD] = key_part.astype(jnp.bfloat16)
            if r > 0:
                copy(2 * s + 1, h, 0, r).start()

    def descend(s, h):
        slot = (2 * s + 1) * KVH + h
        update = jnp.dot(tok_ref[s], gathered[slot], preferred_element_type=jnp.float32)
        scale = jnp.where(
            lax.broadcasted_iota(jnp.int32, (1, 2 * HD), 1) < HD, INNER_RATE, INNER_RATE * VALUE_SCALE
        )
        return theta[h] - update * scale

    def weights(h):
        return jnp.concatenate([w_ref[:, key_cols(h)], w_ref[:, value_cols(h)]], axis=1)

    def finish(h):
        low = weights(h).astype(jnp.float32)
        delta = (low - descend(STEPS - 1, h)).astype(jnp.bfloat16)
        payload = (PAIR_WEIGHT * low - DELTA_WEIGHT * delta.astype(jnp.float32)).astype(jnp.bfloat16)
        delta_ref[:, key_cols(h)] = delta[:, :HD]
        delta_ref[:, value_cols(h)] = delta[:, HD:]
        payload_ref[:, key_cols(h)] = payload[:, :HD]
        payload_ref[:, value_cols(h)] = payload[:, HD:]

    def task(h, index):
        ar, stage = index // 3, index % 3
        if stage == 0:
            if ar > 0:
                arrive(ar - 1, h, 2)
            s = ar // 2
            if ar == 2 * STEPS:
                finish(h)
                return
            if ar % 2 == 1:
                attend(s, h)
                return
            if h == 0:
                if s == 0:
                    loads[0].wait()
                loads[3 * s + 1].wait()
            if s == 0:
                low = weights(h)
                theta[h] = low.astype(jnp.float32)
                project(0, h, low)
            else:
                new = descend(s - 1, h)
                theta[h] = new
                project(s, h, new.astype(jnp.bfloat16))
            if ar == 0 and h == 0:
                pl.semaphore_wait(barrier, 2 * (RING - 1))
            send(ar, h, 0)
            if h == 1:
                loads[3 * s + 2].wait()
                loads[3 * s + 3].wait()
                for other in range(KVH):
                    prepare(s, other)
        elif stage == 1:
            first_sum(ar, h)
        else:
            second_sum(ar, h)

    last = 6 * STEPS
    for tick in range(last + SKEW * (KVH - 1) + 1):
        for h in range(KVH):
            index = tick - SKEW * h
            if 0 <= index <= last:
                task(h, index)


def front(tokens, queries, cotangent, weights_low):
    steps, features, seq = tokens.shape
    columns = weights_low.shape[1]
    lanes = queries.shape[2] // (KVH * HD) * queries.shape[1]
    sums = 2 * steps * KVH
    vmem = pl.BlockSpec(memory_space=pltpu.VMEM)
    out = jax.ShapeDtypeStruct((features, columns), jnp.bfloat16)
    return pl.pallas_call(
        front_kernel,
        out_shape=(out, out),
        in_specs=[pl.BlockSpec(memory_space=pl.ANY)] * 4,
        out_specs=(vmem, vmem),
        scratch_shapes=[
            pltpu.VMEM(tokens.shape, tokens.dtype),
            pltpu.VMEM(queries.shape, queries.dtype),
            pltpu.VMEM(cotangent.shape, cotangent.dtype),
            pltpu.VMEM(weights_low.shape, weights_low.dtype),
            pltpu.VMEM((KVH, features, 2 * HD), jnp.float32),
            pltpu.VMEM((sums, seq, 2 * HD), jnp.bfloat16),
            pltpu.VMEM((sums, seq, 2 * HD), jnp.bfloat16),
            pltpu.VMEM((sums, RING - 1, seq // RING, 2 * HD), jnp.bfloat16),
            pltpu.VMEM((sums, seq // RING, 2 * HD), jnp.bfloat16),
            pltpu.VMEM((sums, RING - 1, seq // RING, 2 * HD), jnp.bfloat16),
            pltpu.VMEM((steps, KVH, lanes, HD), jnp.bfloat16),
            pltpu.VMEM((steps, KVH, lanes, HD), jnp.bfloat16),
            pltpu.VMEM((seq, lanes), jnp.float32),
            pltpu.VMEM((seq, lanes), jnp.float32),
            pltpu.VMEM((seq, HD), jnp.float32),
            pltpu.VMEM((seq, HD), jnp.float32),
            pltpu.SemaphoreType.DMA((3 * STEPS + 1,)),
            pltpu.SemaphoreType.DMA((2, KVH, 3, RING - 1)),
            pltpu.SemaphoreType.DMA((2, KVH, 3, RING - 1)),
        ],
        compiler_params=pltpu.CompilerParams(
            collective_id=0, has_side_effects=True, vmem_limit_bytes=60 * 1024 * 1024
        ),
    )(tokens, queries, cotangent, weights_low)


def from_partner(value, mask_value):
    replicas = lax.axis_size("rep")

    def by(mask, value):
        return lax.ppermute(value, "rep", [(source, source ^ mask) for source in range(replicas)])

    return lax.switch(mask_value - 1, [functools.partial(by, mask) for mask in range(1, replicas)], value)


def on_device(tokens, queries, cotangent, outer_weights, momentum, partner_mask):
    weights_low = outer_weights[0]
    momentum_low = momentum[0]
    payload, weight_delta = front(tokens[0], queries[0], cotangent[0], weights_low)
    partner_payload = from_partner(payload, partner_mask[0])
    outer_full = weights_low.astype(jnp.float32)
    step_change = (
        MOMENTUM_DECAY * momentum_low.astype(jnp.float32)
        - DELTA_WEIGHT * weight_delta.astype(jnp.float32)
        - PAIR_WEIGHT * outer_full
        + partner_payload.astype(jnp.float32)
    )
    return (
        (outer_full + step_change).astype(jnp.bfloat16)[None],
        step_change.astype(jnp.bfloat16)[None],
    )


def solution(mesh):
    in_specs = (
        P("rep", None, ("fsdp", "tp"), None),
        P("rep", None, "fsdp", "tp"),
        P("rep", None, "fsdp", "tp"),
        P("rep", ("fsdp", "tp"), None),
        P("rep", ("fsdp", "tp"), None),
        P(),
    )
    out_specs = (P("rep", ("fsdp", "tp"), None), P("rep", ("fsdp", "tp"), None))
    return jax.shard_map(
        on_device, mesh=mesh, in_specs=in_specs, out_specs=out_specs, check_vma=False
    )
```

```python
import functools

import jax
import jax.numpy as jnp
from jax import lax
from jax.experimental import pallas as pl
from jax.experimental.pallas import tpu as pltpu
from jax.sharding import PartitionSpec as P

D = 5120
HD = 128
KVH = 4
GROUP = 8
STEPS = 2

EPSILON = 1e-06
INNER_RATE = 8.0
MOMENTUM_DECAY = 0.9
DELTA_WEIGHT = 0.35
PAIR_WEIGHT = 0.25

MESH = pl.DeviceIdType.MESH
RING = 4
SKEW = 0
FAR_FIRST = (2, 1, 3)
VALUE_SCALE = D ** (-0.5)
HEAD_SCALE = HD ** (-0.5)


def ring_ids(axis):
    rep, f, t = lax.axis_index("rep"), lax.axis_index("fsdp"), lax.axis_index("tp")
    x, y = t * 2 + f % 2, f // 2
    if axis == 0:
        others = [(x + r) % RING for r in range(1, RING)]
        return x, [(rep, y * 2 + other % 2, other // 2) for other in others]
    others = [(y + r) % RING for r in range(1, RING)]
    return y, [(rep, other * 2 + f % 2, t) for other in others]


def front_kernel(
    tok_hbm,
    query_hbm,
    cot_hbm,
    w_hbm,
    payload_ref,
    delta_ref,
    tok_ref,
    query_ref,
    cot_in_ref,
    w_ref,
    theta,
    gathered,
    staged,
    landed,
    partial,
    crossed,
    query_low,
    cot,
    raised,
    prob_grad,
    units,
    norms,
    load_sem,
    send_sem,
    recv_sem,
):
    seq = tok_ref.shape[2]
    query_rows = query_ref.shape[1]
    groups = query_ref.shape[2] // (KVH * HD)
    lanes = groups * query_rows
    block = seq // RING
    rings = [ring_ids(0), ring_ids(1)]
    first_row = lax.axis_index("fsdp") * query_rows

    pairs = [(w_hbm, w_ref)]
    for s in range(STEPS):
        pairs += [(a.at[s], b.at[s]) for a, b in ((tok_hbm, tok_ref), (query_hbm, query_ref), (cot_hbm, cot_in_ref))]
    loads = [pltpu.make_async_copy(a, b, load_sem.at[i]) for i, (a, b) in enumerate(pairs)]
    for load in loads:
        load.start()

    barrier = pltpu.get_barrier_semaphore()
    for _, ids in rings:
        for other in ids:
            pl.semaphore_signal(barrier, inc=1, device_id=other, device_id_type=MESH)

    def ring(h, phase):
        return rings[(h + phase) % 2]

    def block_rows(h, r=0):
        return pl.ds(pl.multiple_of((ring(h, 0)[0] + r) % RING * block, block), block)

    def copy(ar, h, stage, r):
        slot = ar * KVH + h
        if stage == 0:
            src, dst, phase = staged.at[slot, block_rows(h, r)], landed.at[slot, r - 1], 0
        elif stage == 1:
            src, dst, phase = partial.at[slot], crossed.at[slot, r - 1], 1
        else:
            src = dst = gathered.at[slot, block_rows(h)]
            phase = 0
        return pltpu.make_async_remote_copy(
            src_ref=src,
            dst_ref=dst,
            send_sem=send_sem.at[ar % 2, h, stage, r - 1],
            recv_sem=recv_sem.at[ar % 2, h, stage, r - 1],
            device_id=ring(h, phase)[1][r - 1],
            device_id_type=MESH,
        )

    def send(ar, h, stage):
        for r in FAR_FIRST:
            copy(ar, h, stage, r).start()

    def arrive(ar, h, stage):
        for r in range(1, RING):
            copy(ar, h, stage, r).wait()

    def first_sum(ar, h):
        arrive(ar, h, 0)
        slot = ar * KVH + h
        total = staged[slot, block_rows(h)].astype(jnp.float32)
        for r in range(1, RING):
            total = total + landed[slot, r - 1].astype(jnp.float32)
        partial[slot] = total.astype(jnp.bfloat16)
        send(ar, h, 1)

    def second_sum(ar, h):
        arrive(ar, h, 1)
        slot = ar * KVH + h
        total = partial[slot].astype(jnp.float32)
        for r in range(1, RING):
            total = total + crossed[slot, r - 1].astype(jnp.float32)
        if ar % 2 == 0:
            total = jnp.concatenate([total[:, :HD], total[:, HD:] * VALUE_SCALE], axis=1)
        gathered[slot, block_rows(h)] = total.astype(jnp.bfloat16)
        send(ar, h, 2)

    def key_cols(h):
        return pl.ds(h * HD, HD)

    def value_cols(h):
        return pl.ds(KVH * HD + h * HD, HD)

    def project(s, h, low):
        slot = 2 * s * KVH + h
        staged[slot] = lax.dot_general(
            tok_ref[s], low, (((0,), (0,)), ((), ())), preferred_element_type=jnp.float32
        ).astype(jnp.bfloat16)

    def prepare(s, h):
        for g in range(groups):
            cols = pl.ds((g * KVH + h) * HD, HD)
            q = query_ref[s, :, cols].astype(jnp.float32)
            norm = lax.rsqrt(jnp.mean(q * q, axis=-1, keepdims=True) + EPSILON)
            query_low[s, h, pl.ds(g * query_rows, query_rows)] = (q * norm).astype(jnp.bfloat16)
            cot[s, h, pl.ds(g * query_rows, query_rows)] = cot_in_ref[s, :, cols]

    def attend(s, h):
        slot = 2 * s * KVH + h
        q = query_low[s, h]
        c = cot[s, h]
        contract_last = (((1,), (1,)), ((), ()))
        position = first_row + lax.broadcasted_iota(jnp.int32, (block, lanes), 1) % query_rows
        row = lax.broadcasted_iota(jnp.int32, (block, lanes), 0)
        denom = jnp.zeros((1, lanes), jnp.float32)
        mixed = jnp.zeros((1, lanes), jnp.float32)
        for i in range(RING):
            part = pl.ds(i * block, block)
            keys = gathered[slot, part, :HD].astype(jnp.float32)
            norm = lax.rsqrt(jnp.mean(keys * keys, axis=-1, keepdims=True) + EPSILON)
            unit = keys * norm
            units[part] = unit
            norms[part] = jnp.broadcast_to(norm, unit.shape)
            scores = lax.dot_general(
                unit.astype(jnp.bfloat16), q, contract_last, preferred_element_type=jnp.float32
            )
            e = jnp.where(row + i * block <= position, jnp.exp(scores * HEAD_SCALE), 0.0)
            pg = lax.dot_general(
                gathered[slot, part, HD:], c, contract_last, preferred_element_type=jnp.float32
            )
            denom = denom + jnp.sum(e, axis=0, keepdims=True)
            mixed = mixed + jnp.sum(e * pg, axis=0, keepdims=True)
            raised[part] = e
            prob_grad[part] = pg
        inverse = 1.0 / denom
        mixed = mixed * inverse
        for r in FAR_FIRST + (0,):
            part = block_rows(h, r)
            probs = raised[part] * inverse
            score_low = (probs * (prob_grad[part] - mixed) * HEAD_SCALE).astype(jnp.bfloat16)
            value_part = jnp.dot(probs.astype(jnp.bfloat16), c, preferred_element_type=jnp.float32)
            staged[slot + KVH, part, HD:] = value_part.astype(jnp.bfloat16)
            unit_grad = jnp.dot(score_low, q, preferred_element_type=jnp.float32)
            unit = units[part]
            key_part = (
                unit_grad - unit * jnp.mean(unit_grad * unit, axis=-1, keepdims=True)
            ) * norms[part]
            staged[slot + KVH, part, :HD] = key_part.astype(jnp.bfloat16)
            if r > 0:
                copy(2 * s + 1, h, 0, r).start()

    def descend(s, h):
        slot = (2 * s + 1) * KVH + h
        update = jnp.dot(tok_ref[s], gathered[slot], preferred_element_type=jnp.float32)
        scale = jnp.where(
            lax.broadcasted_iota(jnp.int32, (1, 2 * HD), 1) < HD, INNER_RATE, INNER_RATE * VALUE_SCALE
        )
        return theta[h] - update * scale

    def weights(h):
        return jnp.concatenate([w_ref[:, key_cols(h)], w_ref[:, value_cols(h)]], axis=1)

    def finish(h):
        low = weights(h).astype(jnp.float32)
        delta = (low - descend(STEPS - 1, h)).astype(jnp.bfloat16)
        payload = (PAIR_WEIGHT * low - DELTA_WEIGHT * delta.astype(jnp.float32)).astype(jnp.bfloat16)
        delta_ref[:, key_cols(h)] = delta[:, :HD]
        delta_ref[:, value_cols(h)] = delta[:, HD:]
        payload_ref[:, key_cols(h)] = payload[:, :HD]
        payload_ref[:, value_cols(h)] = payload[:, HD:]

    def task(h, index):
        ar, stage = index // 3, index % 3
        if stage == 0:
            if ar > 0:
                arrive(ar - 1, h, 2)
            s = ar // 2
            if ar == 2 * STEPS:
                finish(h)
                return
            if ar % 2 == 1:
                attend(s, h)
                return
            if h == 0:
                if s == 0:
                    loads[0].wait()
                loads[3 * s + 1].wait()
            if s == 0:
                low = weights(h)
                theta[h] = low.astype(jnp.float32)
                project(0, h, low)
            else:
                new = descend(s - 1, h)
                theta[h] = new
                project(s, h, new.astype(jnp.bfloat16))
            if ar == 0 and h == 0:
                pl.semaphore_wait(barrier, 2 * (RING - 1))
            send(ar, h, 0)
            if h == 1:
                loads[3 * s + 2].wait()
                loads[3 * s + 3].wait()
                for other in range(KVH):
                    prepare(s, other)
        elif stage == 1:
            first_sum(ar, h)
        else:
            second_sum(ar, h)

    last = 6 * STEPS
    for tick in range(last + SKEW * (KVH - 1) + 1):
        for h in range(KVH):
            index = tick - SKEW * h
            if 0 <= index <= last:
                task(h, index)


def front(tokens, queries, cotangent, weights_low):
    steps, features, seq = tokens.shape
    columns = weights_low.shape[1]
    lanes = queries.shape[2] // (KVH * HD) * queries.shape[1]
    sums = 2 * steps * KVH
    vmem = pl.BlockSpec(memory_space=pltpu.VMEM)
    out = jax.ShapeDtypeStruct((features, columns), jnp.bfloat16)
    return pl.pallas_call(
        front_kernel,
        out_shape=(out, out),
        in_specs=[pl.BlockSpec(memory_space=pl.ANY)] * 4,
        out_specs=(vmem, vmem),
        scratch_shapes=[
            pltpu.VMEM(tokens.shape, tokens.dtype),
            pltpu.VMEM(queries.shape, queries.dtype),
            pltpu.VMEM(cotangent.shape, cotangent.dtype),
            pltpu.VMEM(weights_low.shape, weights_low.dtype),
            pltpu.VMEM((KVH, features, 2 * HD), jnp.float32),
            pltpu.VMEM((sums, seq, 2 * HD), jnp.bfloat16),
            pltpu.VMEM((sums, seq, 2 * HD), jnp.bfloat16),
            pltpu.VMEM((sums, RING - 1, seq // RING, 2 * HD), jnp.bfloat16),
            pltpu.VMEM((sums, seq // RING, 2 * HD), jnp.bfloat16),
            pltpu.VMEM((sums, RING - 1, seq // RING, 2 * HD), jnp.bfloat16),
            pltpu.VMEM((steps, KVH, lanes, HD), jnp.bfloat16),
            pltpu.VMEM((steps, KVH, lanes, HD), jnp.bfloat16),
            pltpu.VMEM((seq, lanes), jnp.float32),
            pltpu.VMEM((seq, lanes), jnp.float32),
            pltpu.VMEM((seq, HD), jnp.float32),
            pltpu.VMEM((seq, HD), jnp.float32),
            pltpu.SemaphoreType.DMA((3 * STEPS + 1,)),
            pltpu.SemaphoreType.DMA((2, KVH, 3, RING - 1)),
            pltpu.SemaphoreType.DMA((2, KVH, 3, RING - 1)),
        ],
        compiler_params=pltpu.CompilerParams(
            collective_id=0, has_side_effects=True, vmem_limit_bytes=60 * 1024 * 1024
        ),
    )(tokens, queries, cotangent, weights_low)


def swap_kernel(mask, payload_ref, partner_ref, send_sem, recv_sem):
    other = lax.axis_index("rep")
    for bit in range(lax.axis_size("rep").bit_length() - 1):
        if mask >> bit & 1:
            other = other + (1 - 2 * (lax.axis_index("rep") // 2**bit % 2)) * 2**bit
    partner = (other, lax.axis_index("fsdp"), lax.axis_index("tp"))
    barrier = pltpu.get_barrier_semaphore()
    pl.semaphore_signal(barrier, inc=1, device_id=partner, device_id_type=MESH)
    pl.semaphore_wait(barrier, 1)
    copy = pltpu.make_async_remote_copy(
        src_ref=payload_ref,
        dst_ref=partner_ref,
        send_sem=send_sem,
        recv_sem=recv_sem,
        device_id=partner,
        device_id_type=MESH,
    )
    copy.start()
    copy.wait()


def from_partner(value, mask_value):
    space = pl.BlockSpec(memory_space=pl.ANY)

    def by(mask, value):
        return pl.pallas_call(
            functools.partial(swap_kernel, mask),
            out_shape=jax.ShapeDtypeStruct(value.shape, value.dtype),
            in_specs=[space],
            out_specs=space,
            scratch_shapes=[pltpu.SemaphoreType.DMA, pltpu.SemaphoreType.DMA],
            compiler_params=pltpu.CompilerParams(collective_id=mask, has_side_effects=True),
        )(value)

    replicas = lax.axis_size("rep")
    return lax.switch(mask_value - 1, [functools.partial(by, mask) for mask in range(1, replicas)], value)


def on_device(tokens, queries, cotangent, outer_weights, momentum, partner_mask):
    weights_low = outer_weights[0]
    momentum_low = momentum[0]
    payload, weight_delta = front(tokens[0], queries[0], cotangent[0], weights_low)
    partner_payload = from_partner(payload, partner_mask[0])
    outer_full = weights_low.astype(jnp.float32)
    step_change = (
        MOMENTUM_DECAY * momentum_low.astype(jnp.float32)
        - DELTA_WEIGHT * weight_delta.astype(jnp.float32)
        - PAIR_WEIGHT * outer_full
        + partner_payload.astype(jnp.float32)
    )
    return (
        (outer_full + step_change).astype(jnp.bfloat16)[None],
        step_change.astype(jnp.bfloat16)[None],
    )


def solution(mesh):
    in_specs = (
        P("rep", None, ("fsdp", "tp"), None),
        P("rep", None, "fsdp", "tp"),
        P("rep", None, "fsdp", "tp"),
        P("rep", ("fsdp", "tp"), None),
        P("rep", ("fsdp", "tp"), None),
        P(),
    )
    out_specs = (P("rep", ("fsdp", "tp"), None), P("rep", ("fsdp", "tp"), None))
    return jax.shard_map(
        on_device, mesh=mesh, in_specs=in_specs, out_specs=out_specs, check_vma=False
    )
```

```python
import functools

import jax
import jax.numpy as jnp
from jax import lax
from jax.experimental import pallas as pl
from jax.experimental.pallas import tpu as pltpu
from jax.sharding import PartitionSpec as P

D = 5120
HD = 128
KVH = 4
GROUP = 8
STEPS = 2

EPSILON = 1e-06
INNER_RATE = 8.0
MOMENTUM_DECAY = 0.9
DELTA_WEIGHT = 0.35
PAIR_WEIGHT = 0.25

MESH = pl.DeviceIdType.MESH
RING = 4
SKEW = 0
FAR_FIRST = (2, 1, 3)
VALUE_SCALE = D ** (-0.5)
HEAD_SCALE = HD ** (-0.5)


def ring_ids(axis):
    rep, f, t = lax.axis_index("rep"), lax.axis_index("fsdp"), lax.axis_index("tp")
    x, y = t * 2 + f % 2, f // 2
    if axis == 0:
        others = [(x + r) % RING for r in range(1, RING)]
        return x, [(rep, y * 2 + other % 2, other // 2) for other in others]
    others = [(y + r) % RING for r in range(1, RING)]
    return y, [(rep, other * 2 + f % 2, t) for other in others]


def front_kernel(
    tok_hbm,
    query_hbm,
    cot_hbm,
    w_hbm,
    payload_ref,
    delta_ref,
    tok_ref,
    query_ref,
    cot_in_ref,
    w_ref,
    theta,
    gathered,
    staged,
    landed,
    partial,
    crossed,
    query_low,
    cot,
    raised,
    prob_grad,
    units,
    norms,
    load_sem,
    send_sem,
    recv_sem,
):
    seq = tok_ref.shape[2]
    query_rows = query_ref.shape[1]
    groups = query_ref.shape[2] // (KVH * HD)
    lanes = groups * query_rows
    block = seq // RING
    rings = [ring_ids(0), ring_ids(1)]
    first_row = lax.axis_index("fsdp") * query_rows

    pairs = [(w_hbm, w_ref)]
    for s in range(STEPS):
        pairs += [(a.at[s], b.at[s]) for a, b in ((tok_hbm, tok_ref), (query_hbm, query_ref), (cot_hbm, cot_in_ref))]
    loads = [pltpu.make_async_copy(a, b, load_sem.at[i]) for i, (a, b) in enumerate(pairs)]
    for load in loads:
        load.start()

    barrier = pltpu.get_barrier_semaphore()
    for _, ids in rings:
        for other in ids:
            pl.semaphore_signal(barrier, inc=1, device_id=other, device_id_type=MESH)

    def ring(h, phase):
        return rings[(h + phase) % 2]

    def block_rows(h, r=0):
        return pl.ds(pl.multiple_of((ring(h, 0)[0] + r) % RING * block, block), block)

    def copy(ar, h, stage, r):
        slot = ar * KVH + h
        if stage == 0:
            src, dst, phase = staged.at[slot, block_rows(h, r)], landed.at[slot, r - 1], 0
        elif stage == 1:
            src, dst, phase = partial.at[slot], crossed.at[slot, r - 1], 1
        else:
            src = dst = gathered.at[slot, block_rows(h)]
            phase = 0
        return pltpu.make_async_remote_copy(
            src_ref=src,
            dst_ref=dst,
            send_sem=send_sem.at[ar % 2, h, stage, r - 1],
            recv_sem=recv_sem.at[ar % 2, h, stage, r - 1],
            device_id=ring(h, phase)[1][r - 1],
            device_id_type=MESH,
        )

    def causal(ar, h, stage, r):
        place, last_block = ring(h, 0)[0], rings[1][0]
        ahead, behind = (place + r) % RING, (place + RING - r) % RING
        if ar % 2 == 0 and stage == 2:
            limit_ahead = last_block if h % 2 == 0 else ahead
            return place <= limit_ahead, behind <= last_block
        if ar % 2 == 1 and stage == 0:
            limit_behind = last_block if h % 2 == 0 else behind
            return ahead <= last_block, place <= limit_behind
        return None

    def start(ar, h, stage, r):
        needed = causal(ar, h, stage, r)
        if needed is None:
            copy(ar, h, stage, r).start()
        else:
            pl.when(needed[0])(lambda: copy(ar, h, stage, r).start())

    def send(ar, h, stage):
        for r in FAR_FIRST:
            start(ar, h, stage, r)

    def arrive(ar, h, stage):
        slot = ar * KVH + h
        for r in range(1, RING):
            needed = causal(ar, h, stage, r)
            if needed is None:
                copy(ar, h, stage, r).wait()
                continue
            pl.when(needed[0])(lambda: copy(ar, h, stage, r).wait_send())
            pl.when(needed[1])(lambda: copy(ar, h, stage, r).wait_recv())

            @pl.when(jnp.logical_not(needed[1]))
            def _():
                zeros = jnp.zeros((block, 2 * HD), jnp.bfloat16)
                if stage == 0:
                    landed[slot, r - 1] = zeros
                else:
                    gathered[slot, block_rows(h, RING - r)] = zeros

    def first_sum(ar, h):
        arrive(ar, h, 0)
        slot = ar * KVH + h
        total = staged[slot, block_rows(h)].astype(jnp.float32)
        for r in range(1, RING):
            total = total + landed[slot, r - 1].astype(jnp.float32)
        partial[slot] = total.astype(jnp.bfloat16)
        send(ar, h, 1)

    def second_sum(ar, h):
        arrive(ar, h, 1)
        slot = ar * KVH + h
        total = partial[slot].astype(jnp.float32)
        for r in range(1, RING):
            total = total + crossed[slot, r - 1].astype(jnp.float32)
        if ar % 2 == 0:
            total = jnp.concatenate([total[:, :HD], total[:, HD:] * VALUE_SCALE], axis=1)
        gathered[slot, block_rows(h)] = total.astype(jnp.bfloat16)
        send(ar, h, 2)

    def key_cols(h):
        return pl.ds(h * HD, HD)

    def value_cols(h):
        return pl.ds(KVH * HD + h * HD, HD)

    def project(s, h, low):
        slot = 2 * s * KVH + h
        staged[slot] = lax.dot_general(
            tok_ref[s], low, (((0,), (0,)), ((), ())), preferred_element_type=jnp.float32
        ).astype(jnp.bfloat16)

    def prepare(s, h):
        for g in range(groups):
            cols = pl.ds((g * KVH + h) * HD, HD)
            q = query_ref[s, :, cols].astype(jnp.float32)
            norm = lax.rsqrt(jnp.mean(q * q, axis=-1, keepdims=True) + EPSILON)
            query_low[s, h, pl.ds(g * query_rows, query_rows)] = (q * norm).astype(jnp.bfloat16)
            cot[s, h, pl.ds(g * query_rows, query_rows)] = cot_in_ref[s, :, cols]

    def attend(s, h):
        slot = 2 * s * KVH + h
        q = query_low[s, h]
        c = cot[s, h]
        contract_last = (((1,), (1,)), ((), ()))
        position = first_row + lax.broadcasted_iota(jnp.int32, (block, lanes), 1) % query_rows
        row = lax.broadcasted_iota(jnp.int32, (block, lanes), 0)
        denom = jnp.zeros((1, lanes), jnp.float32)
        mixed = jnp.zeros((1, lanes), jnp.float32)
        for i in range(RING):
            part = pl.ds(i * block, block)
            keys = gathered[slot, part, :HD].astype(jnp.float32)
            norm = lax.rsqrt(jnp.mean(keys * keys, axis=-1, keepdims=True) + EPSILON)
            unit = keys * norm
            units[part] = unit
            norms[part] = jnp.broadcast_to(norm, unit.shape)
            scores = lax.dot_general(
                unit.astype(jnp.bfloat16), q, contract_last, preferred_element_type=jnp.float32
            )
            e = jnp.where(row + i * block <= position, jnp.exp(scores * HEAD_SCALE), 0.0)
            pg = lax.dot_general(
                gathered[slot, part, HD:], c, contract_last, preferred_element_type=jnp.float32
            )
            denom = denom + jnp.sum(e, axis=0, keepdims=True)
            mixed = mixed + jnp.sum(e * pg, axis=0, keepdims=True)
            raised[part] = e
            prob_grad[part] = pg
        inverse = 1.0 / denom
        mixed = mixed * inverse
        for r in FAR_FIRST + (0,):
            part = block_rows(h, r)
            probs = raised[part] * inverse
            score_low = (probs * (prob_grad[part] - mixed) * HEAD_SCALE).astype(jnp.bfloat16)
            value_part = jnp.dot(probs.astype(jnp.bfloat16), c, preferred_element_type=jnp.float32)
            staged[slot + KVH, part, HD:] = value_part.astype(jnp.bfloat16)
            unit_grad = jnp.dot(score_low, q, preferred_element_type=jnp.float32)
            unit = units[part]
            key_part = (
                unit_grad - unit * jnp.mean(unit_grad * unit, axis=-1, keepdims=True)
            ) * norms[part]
            staged[slot + KVH, part, :HD] = key_part.astype(jnp.bfloat16)
            if r > 0:
                start(2 * s + 1, h, 0, r)

    def descend(s, h):
        slot = (2 * s + 1) * KVH + h
        update = jnp.dot(tok_ref[s], gathered[slot], preferred_element_type=jnp.float32)
        scale = jnp.where(
            lax.broadcasted_iota(jnp.int32, (1, 2 * HD), 1) < HD, INNER_RATE, INNER_RATE * VALUE_SCALE
        )
        return theta[h] - update * scale

    def weights(h):
        return jnp.concatenate([w_ref[:, key_cols(h)], w_ref[:, value_cols(h)]], axis=1)

    def finish(h):
        low = weights(h).astype(jnp.float32)
        delta = (low - descend(STEPS - 1, h)).astype(jnp.bfloat16)
        payload = (PAIR_WEIGHT * low - DELTA_WEIGHT * delta.astype(jnp.float32)).astype(jnp.bfloat16)
        delta_ref[:, key_cols(h)] = delta[:, :HD]
        delta_ref[:, value_cols(h)] = delta[:, HD:]
        payload_ref[:, key_cols(h)] = payload[:, :HD]
        payload_ref[:, value_cols(h)] = payload[:, HD:]

    def task(h, index):
        ar, stage = index // 3, index % 3
        if stage == 0:
            if ar > 0:
                arrive(ar - 1, h, 2)
            s = ar // 2
            if ar == 2 * STEPS:
                finish(h)
                return
            if ar % 2 == 1:
                attend(s, h)
                return
            if h == 0:
                if s == 0:
                    loads[0].wait()
                loads[3 * s + 1].wait()
            if s == 0:
                low = weights(h)
                theta[h] = low.astype(jnp.float32)
                project(0, h, low)
            else:
                new = descend(s - 1, h)
                theta[h] = new
                project(s, h, new.astype(jnp.bfloat16))
            if ar == 0 and h == 0:
                pl.semaphore_wait(barrier, 2 * (RING - 1))
            send(ar, h, 0)
            if h == 1:
                loads[3 * s + 2].wait()
                loads[3 * s + 3].wait()
                for other in range(KVH):
                    prepare(s, other)
        elif stage == 1:
            first_sum(ar, h)
        else:
            second_sum(ar, h)

    last = 6 * STEPS
    for tick in range(last + SKEW * (KVH - 1) + 1):
        for h in range(KVH):
            index = tick - SKEW * h
            if 0 <= index <= last:
                task(h, index)


def front(tokens, queries, cotangent, weights_low):
    steps, features, seq = tokens.shape
    columns = weights_low.shape[1]
    lanes = queries.shape[2] // (KVH * HD) * queries.shape[1]
    sums = 2 * steps * KVH
    vmem = pl.BlockSpec(memory_space=pltpu.VMEM)
    out = jax.ShapeDtypeStruct((features, columns), jnp.bfloat16)
    return pl.pallas_call(
        front_kernel,
        out_shape=(out, out),
        in_specs=[pl.BlockSpec(memory_space=pl.ANY)] * 4,
        out_specs=(vmem, vmem),
        scratch_shapes=[
            pltpu.VMEM(tokens.shape, tokens.dtype),
            pltpu.VMEM(queries.shape, queries.dtype),
            pltpu.VMEM(cotangent.shape, cotangent.dtype),
            pltpu.VMEM(weights_low.shape, weights_low.dtype),
            pltpu.VMEM((KVH, features, 2 * HD), jnp.float32),
            pltpu.VMEM((sums, seq, 2 * HD), jnp.bfloat16),
            pltpu.VMEM((sums, seq, 2 * HD), jnp.bfloat16),
            pltpu.VMEM((sums, RING - 1, seq // RING, 2 * HD), jnp.bfloat16),
            pltpu.VMEM((sums, seq // RING, 2 * HD), jnp.bfloat16),
            pltpu.VMEM((sums, RING - 1, seq // RING, 2 * HD), jnp.bfloat16),
            pltpu.VMEM((steps, KVH, lanes, HD), jnp.bfloat16),
            pltpu.VMEM((steps, KVH, lanes, HD), jnp.bfloat16),
            pltpu.VMEM((seq, lanes), jnp.float32),
            pltpu.VMEM((seq, lanes), jnp.float32),
            pltpu.VMEM((seq, HD), jnp.float32),
            pltpu.VMEM((seq, HD), jnp.float32),
            pltpu.SemaphoreType.DMA((3 * STEPS + 1,)),
            pltpu.SemaphoreType.DMA((2, KVH, 3, RING - 1)),
            pltpu.SemaphoreType.DMA((2, KVH, 3, RING - 1)),
        ],
        compiler_params=pltpu.CompilerParams(
            collective_id=0, has_side_effects=True, vmem_limit_bytes=60 * 1024 * 1024
        ),
    )(tokens, queries, cotangent, weights_low)


def swap_kernel(mask, payload_ref, partner_ref, send_sem, recv_sem):
    other = lax.axis_index("rep")
    for bit in range(lax.axis_size("rep").bit_length() - 1):
        if mask >> bit & 1:
            other = other + (1 - 2 * (lax.axis_index("rep") // 2**bit % 2)) * 2**bit
    partner = (other, lax.axis_index("fsdp"), lax.axis_index("tp"))
    barrier = pltpu.get_barrier_semaphore()
    pl.semaphore_signal(barrier, inc=1, device_id=partner, device_id_type=MESH)
    pl.semaphore_wait(barrier, 1)
    copy = pltpu.make_async_remote_copy(
        src_ref=payload_ref,
        dst_ref=partner_ref,
        send_sem=send_sem,
        recv_sem=recv_sem,
        device_id=partner,
        device_id_type=MESH,
    )
    copy.start()
    copy.wait()


def from_partner(value, mask_value):
    space = pl.BlockSpec(memory_space=pl.ANY)

    def by(mask, value):
        return pl.pallas_call(
            functools.partial(swap_kernel, mask),
            out_shape=jax.ShapeDtypeStruct(value.shape, value.dtype),
            in_specs=[space],
            out_specs=space,
            scratch_shapes=[pltpu.SemaphoreType.DMA, pltpu.SemaphoreType.DMA],
            compiler_params=pltpu.CompilerParams(collective_id=mask, has_side_effects=True),
        )(value)

    replicas = lax.axis_size("rep")
    return lax.switch(mask_value - 1, [functools.partial(by, mask) for mask in range(1, replicas)], value)


def on_device(tokens, queries, cotangent, outer_weights, momentum, partner_mask):
    weights_low = outer_weights[0]
    momentum_low = momentum[0]
    payload, weight_delta = front(tokens[0], queries[0], cotangent[0], weights_low)
    partner_payload = from_partner(payload, partner_mask[0])
    outer_full = weights_low.astype(jnp.float32)
    step_change = (
        MOMENTUM_DECAY * momentum_low.astype(jnp.float32)
        - DELTA_WEIGHT * weight_delta.astype(jnp.float32)
        - PAIR_WEIGHT * outer_full
        + partner_payload.astype(jnp.float32)
    )
    return (
        (outer_full + step_change).astype(jnp.bfloat16)[None],
        step_change.astype(jnp.bfloat16)[None],
    )


def solution(mesh):
    in_specs = (
        P("rep", None, ("fsdp", "tp"), None),
        P("rep", None, "fsdp", "tp"),
        P("rep", None, "fsdp", "tp"),
        P("rep", ("fsdp", "tp"), None),
        P("rep", ("fsdp", "tp"), None),
        P(),
    )
    out_specs = (P("rep", ("fsdp", "tp"), None), P("rep", ("fsdp", "tp"), None))
    return jax.shard_map(
        on_device, mesh=mesh, in_specs=in_specs, out_specs=out_specs, check_vma=False
    )
```

```python
import functools

import jax
import jax.numpy as jnp
from jax import lax
from jax.experimental import pallas as pl
from jax.experimental.pallas import tpu as pltpu
from jax.sharding import PartitionSpec as P

D = 5120
HD = 128
KVH = 4
GROUP = 8
STEPS = 2

EPSILON = 1e-06
INNER_RATE = 8.0
MOMENTUM_DECAY = 0.9
DELTA_WEIGHT = 0.35
PAIR_WEIGHT = 0.25

MESH = pl.DeviceIdType.MESH
RING = 4
SKEW = 0
FAR_FIRST = (2, 1, 3)
VALUE_SCALE = D ** (-0.5)
HEAD_SCALE = HD ** (-0.5)


def ring_ids(axis):
    rep, f, t = lax.axis_index("rep"), lax.axis_index("fsdp"), lax.axis_index("tp")
    x, y = t * 2 + f % 2, f // 2
    if axis == 0:
        others = [(x + r) % RING for r in range(1, RING)]
        return x, [(rep, y * 2 + other % 2, other // 2) for other in others]
    others = [(y + r) % RING for r in range(1, RING)]
    return y, [(rep, other * 2 + f % 2, t) for other in others]


def front_kernel(
    tok_hbm,
    query_hbm,
    cot_hbm,
    w_hbm,
    payload_ref,
    delta_ref,
    tok_ref,
    query_ref,
    cot_in_ref,
    w_ref,
    theta,
    gathered,
    staged,
    landed,
    partial,
    crossed,
    query_low,
    cot,
    raised,
    prob_grad,
    units,
    norms,
    load_sem,
    send_sem,
    recv_sem,
):
    seq = tok_ref.shape[2]
    query_rows = query_ref.shape[1]
    groups = query_ref.shape[2] // (KVH * HD)
    lanes = groups * query_rows
    block = seq // RING
    rings = [ring_ids(0), ring_ids(1)]
    first_row = lax.axis_index("fsdp") * query_rows

    pairs = [(w_hbm, w_ref)]
    for s in range(STEPS):
        pairs += [(a.at[s], b.at[s]) for a, b in ((tok_hbm, tok_ref), (query_hbm, query_ref), (cot_hbm, cot_in_ref))]
    loads = [pltpu.make_async_copy(a, b, load_sem.at[i]) for i, (a, b) in enumerate(pairs)]
    for load in loads:
        load.start()

    barrier = pltpu.get_barrier_semaphore()
    for _, ids in rings:
        for other in ids:
            pl.semaphore_signal(barrier, inc=1, device_id=other, device_id_type=MESH)

    def ring(h, phase):
        return rings[(h + phase) % 2]

    def block_rows(h, r=0):
        return pl.ds(pl.multiple_of((ring(h, 0)[0] + r) % RING * block, block), block)

    def copy(ar, h, stage, r):
        slot = ar * KVH + h
        if stage == 0:
            src, dst, phase = staged.at[slot, block_rows(h, r)], landed.at[slot, r - 1], 0
        elif stage == 1:
            src, dst, phase = partial.at[slot], crossed.at[slot, r - 1], 1
        else:
            src = dst = gathered.at[slot, block_rows(h)]
            phase = 0
        return pltpu.make_async_remote_copy(
            src_ref=src,
            dst_ref=dst,
            send_sem=send_sem.at[ar % 2, h, stage, r - 1],
            recv_sem=recv_sem.at[ar % 2, h, stage, r - 1],
            device_id=ring(h, phase)[1][r - 1],
            device_id_type=MESH,
        )

    def causal(ar, h, stage, r):
        place, last_block = ring(h, 0)[0], rings[1][0]
        ahead, behind = (place + r) % RING, (place + RING - r) % RING
        if ar % 2 == 0 and stage == 2:
            limit_ahead = last_block if h % 2 == 0 else ahead
            return place <= limit_ahead, behind <= last_block
        if ar % 2 == 1 and stage == 0:
            limit_behind = last_block if h % 2 == 0 else behind
            return ahead <= last_block, place <= limit_behind
        return None

    def start(ar, h, stage, r):
        needed = causal(ar, h, stage, r)
        if needed is None:
            copy(ar, h, stage, r).start()
        else:
            pl.when(needed[0])(lambda: copy(ar, h, stage, r).start())

    def send(ar, h, stage):
        for r in FAR_FIRST:
            start(ar, h, stage, r)

    def arrive(ar, h, stage):
        slot = ar * KVH + h
        for r in range(1, RING):
            needed = causal(ar, h, stage, r)
            if needed is None:
                copy(ar, h, stage, r).wait()
                continue
            pl.when(needed[0])(lambda: copy(ar, h, stage, r).wait_send())
            pl.when(needed[1])(lambda: copy(ar, h, stage, r).wait_recv())

            @pl.when(jnp.logical_not(needed[1]))
            def _():
                zeros = jnp.zeros((block, 2 * HD), jnp.bfloat16)
                if stage == 0:
                    landed[slot, r - 1] = zeros
                else:
                    gathered[slot, block_rows(h, RING - r)] = zeros

    def first_sum(ar, h):
        arrive(ar, h, 0)
        slot = ar * KVH + h
        total = staged[slot, block_rows(h)].astype(jnp.float32)
        for r in range(1, RING):
            total = total + landed[slot, r - 1].astype(jnp.float32)
        partial[slot] = total.astype(jnp.bfloat16)
        send(ar, h, 1)

    def second_sum(ar, h):
        arrive(ar, h, 1)
        slot = ar * KVH + h
        total = partial[slot].astype(jnp.float32)
        for r in range(1, RING):
            total = total + crossed[slot, r - 1].astype(jnp.float32)
        if ar % 2 == 0:
            total = jnp.concatenate([total[:, :HD], total[:, HD:] * VALUE_SCALE], axis=1)
        gathered[slot, block_rows(h)] = total.astype(jnp.bfloat16)
        send(ar, h, 2)

    def key_cols(h):
        return pl.ds(h * HD, HD)

    def value_cols(h):
        return pl.ds(KVH * HD + h * HD, HD)

    def project(s, h, low):
        slot = 2 * s * KVH + h
        staged[slot] = lax.dot_general(
            tok_ref[s], low, (((0,), (0,)), ((), ())), preferred_element_type=jnp.float32
        ).astype(jnp.bfloat16)

    def prepare(s, h):
        for g in range(groups):
            cols = pl.ds((g * KVH + h) * HD, HD)
            q = query_ref[s, :, cols].astype(jnp.float32)
            norm = lax.rsqrt(jnp.mean(q * q, axis=-1, keepdims=True) + EPSILON)
            query_low[s, h, pl.ds(g * query_rows, query_rows)] = (q * norm).astype(jnp.bfloat16)
            cot[s, h, pl.ds(g * query_rows, query_rows)] = cot_in_ref[s, :, cols]

    def attend(s, h):
        slot = 2 * s * KVH + h
        q = query_low[s, h]
        c = cot[s, h]
        contract_last = (((1,), (1,)), ((), ()))
        position = first_row + lax.broadcasted_iota(jnp.int32, (block, lanes), 1) % query_rows
        row = lax.broadcasted_iota(jnp.int32, (block, lanes), 0)
        denom = jnp.zeros((1, lanes), jnp.float32)
        mixed = jnp.zeros((1, lanes), jnp.float32)
        for i in range(RING):
            part = pl.ds(i * block, block)
            keys = gathered[slot, part, :HD].astype(jnp.float32)
            norm = lax.rsqrt(jnp.mean(keys * keys, axis=-1, keepdims=True) + EPSILON)
            unit = keys * norm
            units[part] = unit
            norms[part] = jnp.broadcast_to(norm, unit.shape)
            scores = lax.dot_general(
                unit.astype(jnp.bfloat16), q, contract_last, preferred_element_type=jnp.float32
            )
            e = jnp.where(row + i * block <= position, jnp.exp(scores * HEAD_SCALE), 0.0)
            pg = lax.dot_general(
                gathered[slot, part, HD:], c, contract_last, preferred_element_type=jnp.float32
            )
            denom = denom + jnp.sum(e, axis=0, keepdims=True)
            mixed = mixed + jnp.sum(e * pg, axis=0, keepdims=True)
            raised[part] = e
            prob_grad[part] = pg
        inverse = 1.0 / denom
        mixed = mixed * inverse
        for r in FAR_FIRST + (0,):
            part = block_rows(h, r)
            probs = raised[part] * inverse
            score_low = (probs * (prob_grad[part] - mixed) * HEAD_SCALE).astype(jnp.bfloat16)
            value_part = jnp.dot(probs.astype(jnp.bfloat16), c, preferred_element_type=jnp.float32)
            staged[slot + KVH, part, HD:] = value_part.astype(jnp.bfloat16)
            unit_grad = jnp.dot(score_low, q, preferred_element_type=jnp.float32)
            unit = units[part]
            key_part = (
                unit_grad - unit * jnp.mean(unit_grad * unit, axis=-1, keepdims=True)
            ) * norms[part]
            staged[slot + KVH, part, :HD] = key_part.astype(jnp.bfloat16)
            if r > 0:
                start(2 * s + 1, h, 0, r)

    def descend(s, h):
        slot = (2 * s + 1) * KVH + h
        update = jnp.dot(tok_ref[s], gathered[slot], preferred_element_type=jnp.float32)
        scale = jnp.where(
            lax.broadcasted_iota(jnp.int32, (1, 2 * HD), 1) < HD, INNER_RATE, INNER_RATE * VALUE_SCALE
        )
        return theta[h] - update * scale

    def weights(h):
        return jnp.concatenate([w_ref[:, key_cols(h)], w_ref[:, value_cols(h)]], axis=1)

    def finish(h):
        low = weights(h).astype(jnp.float32)
        delta = (low - descend(STEPS - 1, h)).astype(jnp.bfloat16)
        payload = (PAIR_WEIGHT * low - DELTA_WEIGHT * delta.astype(jnp.float32)).astype(jnp.bfloat16)
        delta_ref[:, key_cols(h)] = delta[:, :HD]
        delta_ref[:, value_cols(h)] = delta[:, HD:]
        payload_ref[:, key_cols(h)] = payload[:, :HD]
        payload_ref[:, value_cols(h)] = payload[:, HD:]

    def task(h, index):
        ar, stage = index // 3, index % 3
        if stage == 0:
            if ar > 0:
                arrive(ar - 1, h, 2)
            s = ar // 2
            if ar == 2 * STEPS:
                finish(h)
                return
            if ar % 2 == 1:
                attend(s, h)
                return
            if h == 0:
                if s == 0:
                    loads[0].wait()
                loads[3 * s + 1].wait()
            if s == 0:
                low = weights(h)
                theta[h] = low.astype(jnp.float32)
                project(0, h, low)
            else:
                new = descend(s - 1, h)
                theta[h] = new
                project(s, h, new.astype(jnp.bfloat16))
            if ar == 0 and h == 0:
                pl.semaphore_wait(barrier, 2 * (RING - 1))
            send(ar, h, 0)
            if s == 0 and h in (1, KVH - 1):
                ahead = h // (KVH - 1)
                loads[3 * ahead + 2].wait()
                loads[3 * ahead + 3].wait()
                for other in range(KVH):
                    prepare(ahead, other)
        elif stage == 1:
            first_sum(ar, h)
        else:
            second_sum(ar, h)

    last = 6 * STEPS
    for tick in range(last + SKEW * (KVH - 1) + 1):
        for h in range(KVH):
            index = tick - SKEW * h
            if 0 <= index <= last:
                task(h, index)


def front(tokens, queries, cotangent, weights_low):
    steps, features, seq = tokens.shape
    columns = weights_low.shape[1]
    lanes = queries.shape[2] // (KVH * HD) * queries.shape[1]
    sums = 2 * steps * KVH
    vmem = pl.BlockSpec(memory_space=pltpu.VMEM)
    out = jax.ShapeDtypeStruct((features, columns), jnp.bfloat16)
    return pl.pallas_call(
        front_kernel,
        out_shape=(out, out),
        in_specs=[pl.BlockSpec(memory_space=pl.ANY)] * 4,
        out_specs=(vmem, vmem),
        scratch_shapes=[
            pltpu.VMEM(tokens.shape, tokens.dtype),
            pltpu.VMEM(queries.shape, queries.dtype),
            pltpu.VMEM(cotangent.shape, cotangent.dtype),
            pltpu.VMEM(weights_low.shape, weights_low.dtype),
            pltpu.VMEM((KVH, features, 2 * HD), jnp.float32),
            pltpu.VMEM((sums, seq, 2 * HD), jnp.bfloat16),
            pltpu.VMEM((sums, seq, 2 * HD), jnp.bfloat16),
            pltpu.VMEM((sums, RING - 1, seq // RING, 2 * HD), jnp.bfloat16),
            pltpu.VMEM((sums, seq // RING, 2 * HD), jnp.bfloat16),
            pltpu.VMEM((sums, RING - 1, seq // RING, 2 * HD), jnp.bfloat16),
            pltpu.VMEM((steps, KVH, lanes, HD), jnp.bfloat16),
            pltpu.VMEM((steps, KVH, lanes, HD), jnp.bfloat16),
            pltpu.VMEM((seq, lanes), jnp.float32),
            pltpu.VMEM((seq, lanes), jnp.float32),
            pltpu.VMEM((seq, HD), jnp.float32),
            pltpu.VMEM((seq, HD), jnp.float32),
            pltpu.SemaphoreType.DMA((3 * STEPS + 1,)),
            pltpu.SemaphoreType.DMA((2, KVH, 3, RING - 1)),
            pltpu.SemaphoreType.DMA((2, KVH, 3, RING - 1)),
        ],
        compiler_params=pltpu.CompilerParams(
            collective_id=0, has_side_effects=True, vmem_limit_bytes=60 * 1024 * 1024
        ),
    )(tokens, queries, cotangent, weights_low)


def swap_kernel(mask, payload_ref, partner_ref, send_sem, recv_sem):
    other = lax.axis_index("rep")
    for bit in range(lax.axis_size("rep").bit_length() - 1):
        if mask >> bit & 1:
            other = other + (1 - 2 * (lax.axis_index("rep") // 2**bit % 2)) * 2**bit
    partner = (other, lax.axis_index("fsdp"), lax.axis_index("tp"))
    barrier = pltpu.get_barrier_semaphore()
    pl.semaphore_signal(barrier, inc=1, device_id=partner, device_id_type=MESH)
    pl.semaphore_wait(barrier, 1)
    copy = pltpu.make_async_remote_copy(
        src_ref=payload_ref,
        dst_ref=partner_ref,
        send_sem=send_sem,
        recv_sem=recv_sem,
        device_id=partner,
        device_id_type=MESH,
    )
    copy.start()
    copy.wait()


def from_partner(value, mask_value):
    space = pl.BlockSpec(memory_space=pl.ANY)

    def by(mask, value):
        return pl.pallas_call(
            functools.partial(swap_kernel, mask),
            out_shape=jax.ShapeDtypeStruct(value.shape, value.dtype),
            in_specs=[space],
            out_specs=space,
            scratch_shapes=[pltpu.SemaphoreType.DMA, pltpu.SemaphoreType.DMA],
            compiler_params=pltpu.CompilerParams(collective_id=mask, has_side_effects=True),
        )(value)

    replicas = lax.axis_size("rep")
    return lax.switch(mask_value - 1, [functools.partial(by, mask) for mask in range(1, replicas)], value)


def on_device(tokens, queries, cotangent, outer_weights, momentum, partner_mask):
    weights_low = outer_weights[0]
    momentum_low = momentum[0]
    payload, weight_delta = front(tokens[0], queries[0], cotangent[0], weights_low)
    partner_payload = from_partner(payload, partner_mask[0])
    outer_full = weights_low.astype(jnp.float32)
    step_change = (
        MOMENTUM_DECAY * momentum_low.astype(jnp.float32)
        - DELTA_WEIGHT * weight_delta.astype(jnp.float32)
        - PAIR_WEIGHT * outer_full
        + partner_payload.astype(jnp.float32)
    )
    return (
        (outer_full + step_change).astype(jnp.bfloat16)[None],
        step_change.astype(jnp.bfloat16)[None],
    )


def solution(mesh):
    in_specs = (
        P("rep", None, ("fsdp", "tp"), None),
        P("rep", None, "fsdp", "tp"),
        P("rep", None, "fsdp", "tp"),
        P("rep", ("fsdp", "tp"), None),
        P("rep", ("fsdp", "tp"), None),
        P(),
    )
    out_specs = (P("rep", ("fsdp", "tp"), None), P("rep", ("fsdp", "tp"), None))
    return jax.shard_map(
        on_device, mesh=mesh, in_specs=in_specs, out_specs=out_specs, check_vma=False
    )
```
